256 devices in a mesh: tg: 4 (over y), pl: 64 (over x, z, core).
Axes of the slice: x: 4, y: 4, z: 8, core: 2. Of those that a mesh axis runs over, the one named last changes fastest.
Arguments:
- coeffs: float32 [2, 4, 8192, 128], P(None, None, ('tg', 'pl')), may hold values from -6 to 6
- potential: float32 [256, 256, 256], P('pl'), may hold values from -2 to 1
- stick_x: int32 [8192], P(('tg', 'pl')), may hold values from 0 to 255, as said below
- stick_y: int32 [8192], P(('tg', 'pl')), may hold values from 0 to 255, as said below
- stick_count: int32 [8192], P(('tg', 'pl')), may hold values from 0 to 128, as said below
- stick_offset: int32 [8192], P(('tg', 'pl')), may hold values from 0 to 255, as said below
Outputs:
- hpsi: float32 [2, 4, 8192, 128], P(None, None, ('tg', 'pl'))
The draws below stay inside these ranges and needn't reach their ends.
Inputs may be any that keep to these rules, and one draw needn't show every extreme that they name: The columns stick_x * 256 + stick_y of all 8192 sticks are distinct. `stick_y`: a stick with count 1 or more has signed column frequencies fx, fy with fx^2 + fy^2 <= 64^2; a stick with count 0 lies outside that disk. `stick_count`: a live stick's count is min(128, 2 * floor(sqrt(64^2 - fx^2 - fy^2)) + 1); on each device's 32 slots the live sticks come first; one device has all 32 slots live and its first stick is the column (0, 0) with 128 G-vectors; every other device has between 16 and 20 live sticks. stick_offset = (-(stick_count // 2)) mod 256, so each stick's G-vectors are centred on z = 0.
All inputs are finite; a program needn't handle non-finite values.
Results may differ from the reference program's by a relative error of at most 0.0002.
Values sent between devices are 32-bit elements; how exact they have to be, the bound alone decides.
A program may use at most 128 MiB of HBM per device.

```python
import math
import jax
import jax.numpy as jnp
import numpy as np
from jax import lax

NG = 256
ZMAX = 128
SLOT = 32
BANDS = 4
STICKS = 8192


def sphere_tables():
    radius = NG // 4
    grid_ids = np.arange(NG)
    signed = np.where(grid_ids < NG // 2, grid_ids, grid_ids - NG)
    freq_x = np.repeat(signed, NG)
    freq_y = np.tile(signed, NG)
    column = np.arange(NG * NG)
    radial = freq_x * freq_x + freq_y * freq_y
    inside = radial <= radius * radius
    remain = np.maximum(radius * radius - radial, 0)
    steps_up = np.arange(1, radius + 1)
    root_val = (steps_up[None, :] * steps_up[None, :] <= remain[:, None]).sum(axis=1)
    heights = np.minimum(ZMAX, 2 * root_val + 1)
    others = inside & (column != 0)
    inside_cols = np.concatenate([np.array([0]), column[others]]).astype(np.int32)
    inside_counts = np.concatenate([np.array([min(ZMAX, 2 * radius + 1)]), heights[others]]).astype(np.int32)
    outside_cols = column[~inside].astype(np.int32)
    return (jnp.asarray(inside_cols), jnp.asarray(inside_counts), jnp.asarray(outside_cols))


def sphere_sticks(key):
    inside_cols, inside_counts, outside_cols = sphere_tables()
    key = jax.random.fold_in(key, 11)
    key_live, key_busy, key_inner, key_outer = jax.random.split(key, 4)
    devices = STICKS // SLOT
    live_count = jax.random.randint(key_live, (devices,), SLOT // 2, SLOT * 5 // 8 + 1)
    busiest = jax.random.randint(key_busy, (), 0, devices)
    device_ids = jnp.arange(devices, dtype=jnp.int32)
    live_count = jnp.where(device_ids == busiest, SLOT, live_count)
    slot_ids = jnp.arange(SLOT, dtype=jnp.int32)
    live = (slot_ids[None, :] < live_count[:, None]).astype(jnp.int32)
    rolled = jnp.roll(live, -busiest, axis=0).reshape(-1)
    live_rank = jnp.maximum(jnp.cumsum(rolled) - 1, 0)
    dead_rank = jnp.maximum(jnp.cumsum(1 - rolled) - 1, 0)
    inner_order = jnp.concatenate([jnp.zeros((1,), jnp.int32), 1 + jax.random.permutation(key_inner, inside_cols.shape[0] - 1).astype(jnp.int32)])
    outer_order = jax.random.permutation(key_outer, outside_cols.shape[0]).astype(jnp.int32)
    picked = inner_order[live_rank]
    col_live = inside_cols[picked]
    cnt_live = inside_counts[picked]
    col_dead = outside_cols[outer_order[dead_rank]]
    column = jnp.where(rolled == 1, col_live, col_dead)
    height = jnp.where(rolled == 1, cnt_live, 0)
    column = jnp.roll(column.reshape(devices, SLOT), busiest, axis=0).reshape(-1)
    height = jnp.roll(height.reshape(devices, SLOT), busiest, axis=0).reshape(-1)
    return (column.astype(jnp.int32), height.astype(jnp.int32))


def draw_stick_x(key, part):
    column, height = sphere_sticks(key)
    return (column // NG).astype(jnp.int32)


def draw_stick_y(key, part):
    column, height = sphere_sticks(key)
    return (column % NG).astype(jnp.int32)


def draw_stick_count(key, part):
    column, height = sphere_sticks(key)
    return height


def draw_stick_offset(key, part):
    column, height = sphere_sticks(key)
    return (-(height // 2) % NG).astype(jnp.int32)


def levels(key, extent, cuts, smallest, largest):
    loudness = 1.0
    for axis_at, blocks in cuts:
        steps = jax.random.uniform(jax.random.fold_in(jax.random.fold_in(key, 6), axis_at), (blocks,), jnp.float32, smallest / len(cuts), largest / len(cuts))
        loudness = loudness * jnp.repeat(jnp.exp(steps), extent[axis_at] // blocks).reshape((-1,) + (1,) * (len(extent) - 1 - axis_at))
    return loudness


def gaussian(own_key, shape, spread, bound, shards=(), kind=jnp.bfloat16):
    values = jax.random.normal(own_key, shape, jnp.float32) * spread
    if len(shards) > 0:
        values = levels(own_key, shape, shards, -0.22, 0.18) * values
    return jnp.clip(values, min=-bound, max=bound).astype(kind)


def setup_inputs(seed: int = 0) -> dict:
    splits = jax.random.split(jax.random.key(seed), 7)
    return {
        "coeffs": gaussian(splits[0], (2, BANDS, STICKS, ZMAX), 1.0, 6.0, ((2, 256),), jnp.float32),
        "potential": jnp.clip(-2.0 + 3.0 * jax.random.uniform(splits[1], (NG, NG, NG), jnp.float32) ** levels(splits[1], (NG, NG, NG), ((0, 64),), -0.2, 0.2), -2.0, 1.0),
        "stick_x": draw_stick_x(jax.random.fold_in(splits[6], 71), 0),
        "stick_y": draw_stick_y(jax.random.fold_in(splits[6], 71), 0),
        "stick_count": draw_stick_count(jax.random.fold_in(splits[6], 71), 0),
        "stick_offset": draw_stick_offset(jax.random.fold_in(splits[6], 71), 0),
    }


def signed_freq(indices):
    return jnp.where(indices < NG // 2, indices, indices - NG)


def trig_tables():
    row_ids = jnp.arange(NG, dtype=jnp.int32)[:, None]
    col_ids = jnp.arange(NG, dtype=jnp.int32)[None, :]
    angle = ((row_ids * col_ids) % NG).astype(jnp.float32) * (2.0 * math.pi / NG)
    return jnp.cos(angle), jnp.sin(angle)


def along_axis(field_re, field_im, cos_tab, sin_tab, direction, form):
    apply = lambda table, field: jnp.einsum(form, table, field, precision=lax.Precision.HIGHEST)
    out_re = apply(cos_tab, field_re) - direction * apply(sin_tab, field_im)
    out_im = apply(cos_tab, field_im) + direction * apply(sin_tab, field_re)
    return out_re, out_im


def transform(field_re, field_im, direction):
    cos_tab, sin_tab = trig_tables()
    field_re, field_im = along_axis(field_re, field_im, cos_tab, sin_tab, direction, 'gz,gxy->zxy')
    field_re, field_im = along_axis(field_re, field_im, cos_tab, sin_tab, direction, 'gx,zgy->zxy')
    field_re, field_im = along_axis(field_re, field_im, cos_tab, sin_tab, direction, 'gy,zxg->zxy')
    return field_re, field_im


def reference(coeffs, potential, stick_x, stick_y, stick_count, stick_offset):
    depth_ids = jnp.arange(ZMAX, dtype=jnp.int32)
    z_index = (stick_offset[:, None] + depth_ids[None, :]) % NG
    x_index = jnp.broadcast_to(stick_x[:, None], z_index.shape)
    y_index = jnp.broadcast_to(stick_y[:, None], z_index.shape)
    live_mask = jnp.where(depth_ids[None, :] < stick_count[:, None], 1.0, 0.0).astype(coeffs.dtype)
    squared = signed_freq(x_index) ** 2 + signed_freq(y_index) ** 2 + signed_freq(z_index) ** 2
    kinetic = 0.5 * (32.0 / (NG * NG)) * squared.astype(coeffs.dtype)
    volume = float(NG) ** 3

    def one_band(band_coef):
        coef_re = band_coef[0] * live_mask
        coef_im = band_coef[1] * live_mask
        grid_re = jnp.zeros((NG, NG, NG), coeffs.dtype).at[z_index, x_index, y_index].add(coef_re)
        grid_im = jnp.zeros((NG, NG, NG), coeffs.dtype).at[z_index, x_index, y_index].add(coef_im)
        spatial_re, spatial_im = transform(grid_re, grid_im, 1.0)
        recip_re, recip_im = transform(potential * spatial_re, potential * spatial_im, -1.0)
        picked_re = recip_re[z_index, x_index, y_index] / volume
        picked_im = recip_im[z_index, x_index, y_index] / volume
        out_re = (picked_re + kinetic * coef_re) * live_mask
        out_im = (picked_im + kinetic * coef_im) * live_mask
        return jnp.stack([out_re, out_im])

    results = lax.map(one_band, jnp.transpose(coeffs, (1, 0, 2, 3)))
    return jnp.transpose(results, (1, 0, 2, 3))
```

```python
import functools
import math

import jax
import jax.numpy as jnp
import numpy as np
from jax import lax
from jax.experimental import pallas as pl
from jax.experimental.pallas import tpu as pltpu
from jax.sharding import PartitionSpec as P

BF = jnp.bfloat16
F32 = jnp.float32
MESH = pl.DeviceIdType.MESH

NG = 256
DEPTH = 128
SLOT = 32
GROUPS = 4
PLANES = 64
LAYERS = 4
ROWS = 2 * LAYERS
KEPT = 128
STEP = 8


def halves(table):
    import ml_dtypes

    high = table.astype(ml_dtypes.bfloat16)
    low = (table - high.astype(np.float64)).astype(ml_dtypes.bfloat16)
    return np.stack([high, low])


def angles(rows, cols):
    return (np.multiply.outer(rows, cols) % NG) * (2.0 * math.pi / NG)


@functools.lru_cache(None)
def tables():
    angle = angles(np.arange(NG), np.arange(DEPTH)).reshape(PLANES, LAYERS, DEPTH)
    cos, sin = np.cos(angle), np.sin(angle)
    real = np.concatenate([cos, -sin], -1)
    imag = np.concatenate([sin, cos], -1)
    straight = np.concatenate([real, imag], 1).reshape(-1, 2 * DEPTH)
    turned = np.concatenate([-imag, real], 1).reshape(-1, 2 * DEPTH)
    lines = np.concatenate([straight, turned])
    angle = angles(np.arange(NG), np.arange(NG)).reshape(PLANES, LAYERS, NG)
    double = lambda t: np.concatenate([t, t], 1).reshape(-1, NG)
    phase = np.concatenate([double(np.cos(angle)), double(np.sin(angle))])
    freq = np.arange(KEPT) - KEPT // 2
    split = np.concatenate([freq[0::2], freq[1::2]])
    angle = angles(np.arange(NG), split)
    cos, sin = np.cos(angle), np.sin(angle)
    along_x = np.block([[cos, -sin], [sin, cos]])
    angle = angles(freq, np.arange(NG))
    cos, sin = np.cos(angle), np.sin(angle)
    along_y = np.block([[cos, sin], [-sin, cos]])
    scale = 1.0 / float(NG) ** 3
    return tuple(
        halves(t)
        for t in (lines, lines.T * scale, phase, along_x, along_x.T, along_y, along_y.T)
    )


def split(values):
    high = values.astype(BF)
    return high, (values - high.astype(F32)).astype(BF)


def dot(a, b):
    return jnp.dot(a, b, preferred_element_type=F32)


def dot3(a, b):
    return dot(a[0], b[0]) + (dot(a[0], b[1]) + dot(a[1], b[0]))


def quarter(index):
    index = index & 3
    one, zero = jnp.float32(1.0), jnp.float32(0.0)
    cos = jnp.where(index == 0, one, jnp.where(index == 2, -one, zero))
    sin = jnp.where(index == 1, one, jnp.where(index == 3, -one, zero))
    return cos, sin


def kernel(
    coeffs,
    meta,
    potential,
    lines_hbm,
    lines_t_hbm,
    phase_hbm,
    ax_hbm,
    axt_hbm,
    ay_hbm,
    ayt_hbm,
    result,
    group,
    metas,
    pot,
    lines,
    lines_t,
    phase,
    ax,
    axt,
    ay,
    ayt,
    send,
    recv,
    phases,
    onehot,
    spread,
    plane,
    psi,
    fields,
    sback,
    ret,
    back,
    local_sem,
    tg_send,
    tg_recv,
    out_send,
    out_recv,
    meta_send,
    meta_recv,
    pl_send,
    pl_recv,
    rt_send,
    rt_recv,
):
    tg = lax.axis_index("tg")
    me = lax.axis_index("pl")
    fetches = [
        pltpu.make_async_copy(src, dst, local_sem.at[i])
        for i, (src, dst) in enumerate(
            [
                (coeffs.at[:, tg], group.at[:, tg]),
                (phase_hbm, phase),
                (lines_hbm, lines),
                (ax_hbm, ax),
                (ay_hbm, ay),
                (potential, pot),
                (ayt_hbm, ayt),
                (axt_hbm, axt),
                (lines_t_hbm, lines_t),
            ]
        )
    ]
    for fetch in fetches:
        fetch.start()

    barrier = pltpu.get_barrier_semaphore()
    for step in range(1, GROUPS):
        pl.semaphore_signal(
            barrier, inc=1, device_id=(lax.rem(tg + step, GROUPS), me), device_id_type=MESH
        )

    def greet(step, carry):
        pl.semaphore_signal(
            barrier, inc=1, device_id=(tg, lax.rem(me + step, PLANES)), device_id_type=MESH
        )
        return carry

    lax.fori_loop(1, PLANES, greet, 0)
    pl.semaphore_wait(barrier, GROUPS - 1 + PLANES - 1)

    copies = []
    for step in range(1, GROUPS):
        other = lax.rem(tg + step, GROUPS)
        for src, dst, sems in (
            (meta, metas.at[step], (meta_send, meta_recv)),
            (coeffs.at[:, other], group.at[:, tg], (tg_send, tg_recv)),
        ):
            copy = pltpu.make_async_remote_copy(
                src_ref=src,
                dst_ref=dst,
                send_sem=sems[0].at[step],
                recv_sem=sems[1].at[step],
                device_id=(other, me),
                device_id_type=MESH,
            )
            copy.start()
            copies.append(copy)
    for copy in copies[0::2]:
        copy.wait()
    info = meta[...] + metas[1] + metas[2] + metas[3]
    ids, count, offset = info[0:1], info[1:2], info[2:3]
    fetches[1].wait()
    steps = lax.broadcasted_iota(jnp.int32, (NG, 128), 0).astype(F32)
    chosen = jnp.where(steps == offset, 1.0, 0.0).astype(BF)
    phases[...] = dot(phase[0], chosen) + dot(phase[1], chosen)
    fetches[0].wait()
    fetches[2].wait()
    for copy in copies[1::2]:
        copy.wait()

    live = steps[:DEPTH] < count
    parts = []
    for part in range(2):
        rows = group[part].reshape(GROUPS * SLOT, DEPTH)
        parts.append(jnp.where(live, rows.T, 0.0))
    both = dot3((lines[0], lines[1]), split(jnp.concatenate(parts, 0)))
    moved = both[: PLANES * ROWS] * phases[: PLANES * ROWS]
    moved = moved + both[PLANES * ROWS :] * phases[PLANES * ROWS :]
    send[:, 0:ROWS, :] = moved.reshape(PLANES, ROWS, 128)
    send[:, ROWS : ROWS + 1, :] = jnp.broadcast_to(ids[None], (PLANES, 1, 128))

    def outgoing(step):
        other = lax.rem(me + step, PLANES)
        return pltpu.make_async_remote_copy(
            src_ref=send.at[other],
            dst_ref=recv.at[step],
            send_sem=pl_send.at[step],
            recv_sem=pl_recv.at[step],
            device_id=(tg, other),
            device_id_type=MESH,
        )

    def launch(step, carry):
        outgoing(step).start()
        return carry

    lax.fori_loop(1, PLANES, launch, 0)
    recv[0] = send[me]

    column = lax.broadcasted_iota(jnp.int32, (2 * KEPT, 128), 0).astype(F32).astype(BF)
    second = jnp.where(lax.broadcasted_iota(jnp.int32, (16, 128), 0) >= 8, 1.0, 0.0).astype(F32)
    one, zero = jnp.ones((), BF), jnp.zeros((), BF)

    def place(g, carry):
        def arrive(i, carry):
            outgoing(g * STEP + i).wait_recv()
            return carry

        lax.fori_loop(jnp.where(g == 0, 1, 0), STEP, arrive, 0)
        block = recv[pl.ds(g * STEP, STEP)]
        left, right = [], []
        for i in range(STEP):
            high, low = split(block[i, 0:ROWS])
            row = block[i, ROWS : ROWS + 1]
            upper = jnp.floor(row * (1.0 / 256.0))
            lower = (row - 256.0 * upper).astype(BF)
            match = (upper - second).astype(BF)
            pieces = []
            for value in (high, low):
                value = jnp.concatenate([value, value], 0)
                for j in range(KEPT // 4):
                    pieces.append(jnp.where(match == jnp.asarray(2.0 * j, BF), value, zero))
            left.append(jnp.concatenate(pieces, 0))
            right.append(jnp.where(column == lower, one, zero))
        left = jnp.concatenate(left, 1)
        right = jnp.concatenate(right, 1)
        onehot[g] = right
        total = lax.dot_general(
            left, right, (((1,), (1,)), ((), ())), preferred_element_type=F32
        )
        half = KEPT // 2 * ROWS
        total = total[:half] + total[half:]

        @pl.when(g == 0)
        def _():
            spread[0] = total[:, :KEPT]
            spread[1] = total[:, KEPT:]

        @pl.when(g > 0)
        def _():
            spread[0] += total[:, :KEPT]
            spread[1] += total[:, KEPT:]

        return carry

    lax.fori_loop(0, PLANES // STEP, place, 0)

    corner = spread[0, 0:ROWS]
    lane = lax.broadcasted_iota(jnp.int32, (ROWS, 128), 1)
    edge_x = jnp.where(lane == 0, corner, 0.0).sum(axis=1, keepdims=True)
    edge_y = jnp.where(lane == 1, corner, 0.0).sum(axis=1, keepdims=True)
    spread[0, 0:ROWS] = jnp.where(lane < 2, 0.0, corner)
    fetches[3].wait()
    columns = []
    for z in range(LAYERS):
        stack = []
        for part in range(2):
            for parity in range(2):
                stack.append(spread[parity, pl.ds(part * LAYERS + z, KEPT // 2, stride=ROWS), :])
        columns.append(jnp.concatenate(stack, 0))
    mixed = dot3((ax[0], ax[1]), split(jnp.concatenate(columns, 1)))
    fields[...] = mixed

    fetches[4].wait()
    fetches[5].wait()
    fetches[6].wait()
    cos_x, sin_x = quarter(lax.broadcasted_iota(jnp.int32, (NG, KEPT), 0))
    cos_y, sin_y = quarter(lax.broadcasted_iota(jnp.int32, (1, NG), 1))
    row_id = lax.broadcasted_iota(jnp.int32, (ROWS, 128), 0)
    got_x = jnp.zeros((ROWS, 128), F32)
    got_y = jnp.zeros((ROWS, 128), F32)
    centre = lax.broadcasted_iota(jnp.int32, (1, KEPT), 1) == KEPT // 2
    for z in range(LAYERS):
        re = fields[0:NG, z * KEPT : (z + 1) * KEPT]
        im = fields[NG : 2 * NG, z * KEPT : (z + 1) * KEPT]
        er = jnp.where(centre, edge_x[z : z + 1], 0.0)
        ei = jnp.where(centre, edge_x[LAYERS + z : LAYERS + z + 1], 0.0)
        re = re + (cos_x * er - sin_x * ei)
        im = im + (sin_x * er + cos_x * ei)
        wave = dot3(split(jnp.concatenate([re, im], 1)), (ay[0], ay[1]))
        er = edge_y[z : z + 1]
        ei = edge_y[LAYERS + z : LAYERS + z + 1]
        local = pot[z]
        re = (wave[:, :NG] + (cos_y * er - sin_y * ei)) * local
        im = (wave[:, NG:] + (sin_y * er + cos_y * ei)) * local
        sum_re = re.sum(axis=0, keepdims=True)
        sum_im = im.sum(axis=0, keepdims=True)
        er = (cos_y * sum_re + sin_y * sum_im).sum(axis=1, keepdims=True)
        ei = (cos_y * sum_im - sin_y * sum_re).sum(axis=1, keepdims=True)
        got_y = jnp.where(row_id == z, er, jnp.where(row_id == LAYERS + z, ei, got_y))
        mid = dot3(split(jnp.concatenate([re, im], 1)), (ayt[0], ayt[1]))
        re, im = mid[:, :KEPT], mid[:, KEPT:]
        er = (cos_x * re + sin_x * im).sum(axis=0, keepdims=True)
        ei = (cos_x * im - sin_x * re).sum(axis=0, keepdims=True)
        er = jnp.where(centre, er, 0.0).sum(axis=1, keepdims=True)
        ei = jnp.where(centre, ei, 0.0).sum(axis=1, keepdims=True)
        got_x = jnp.where(row_id == z, er, jnp.where(row_id == LAYERS + z, ei, got_x))
        fields[0:NG, z * KEPT : (z + 1) * KEPT] = re
        fields[NG : 2 * NG, z * KEPT : (z + 1) * KEPT] = im
    fetches[7].wait()
    mixed = dot3((axt[0], axt[1]), split(fields[...]))
    for z in range(LAYERS):
        for part in range(2):
            block = mixed[part * KEPT : (part + 1) * KEPT, z * KEPT : (z + 1) * KEPT]
            for parity in range(2):
                plane[parity, pl.ds(part * LAYERS + z, KEPT // 2, stride=ROWS), :] = block[
                    parity * (KEPT // 2) : (parity + 1) * (KEPT // 2)
                ]
    corner = plane[0, 0:ROWS]
    plane[0, 0:ROWS] = jnp.where(lane == 0, got_x, jnp.where(lane == 1, got_y, corner))
    for parity in range(2):
        high, low = split(plane[parity])
        psi[:, parity * KEPT : (parity + 1) * KEPT] = high
        psi[:, (2 + parity) * KEPT : (3 + parity) * KEPT] = low

    def incoming(step):
        other = lax.rem(me - step + PLANES, PLANES)
        return pltpu.make_async_remote_copy(
            src_ref=sback.at[step],
            dst_ref=ret.at[me],
            send_sem=rt_send.at[step],
            recv_sem=rt_recv.at[step],
            device_id=(tg, other),
            device_id_type=MESH,
        )

    def pick(g, carry):
        for i in range(STEP):
            right = onehot[g, :, i * 128 : (i + 1) * 128]
            found = dot(psi[...], jnp.concatenate([right, right], 0))
            row = recv[g * STEP + i, ROWS : ROWS + 1]
            upper = jnp.broadcast_to(jnp.floor(row * (1.0 / 256.0)), (ROWS, 128))
            value = jnp.zeros((ROWS, 128), F32)
            for j in range(KEPT // 2):
                value = jnp.where(upper == float(j), found[j * ROWS : (j + 1) * ROWS], value)
            sback[g * STEP + i] = value

        def leave(i, carry):
            incoming(g * STEP + i).start()
            return carry

        lax.fori_loop(jnp.where(g == 0, 1, 0), STEP, leave, 0)
        return carry

    lax.fori_loop(0, PLANES // STEP, pick, 0)
    ret[me] = sback[0]

    def settle(step, carry):
        incoming(step).wait_recv()
        return carry

    lax.fori_loop(1, PLANES, settle, 0)
    fetches[8].wait()
    arrived = ret[...].reshape(PLANES * ROWS, 128)
    pair = jnp.concatenate(
        [arrived * phases[: PLANES * ROWS], arrived * phases[PLANES * ROWS :]], 0
    )
    picked = dot3((lines_t[0], lines_t[1]), split(pair))
    for part in range(2):
        rows = picked[part * DEPTH : (part + 1) * DEPTH].T
        back[part] = rows.reshape(GROUPS, SLOT, DEPTH)

    copies = []
    for step in range(1, GROUPS):
        other = lax.rem(tg + step, GROUPS)
        copy = pltpu.make_async_remote_copy(
            src_ref=back.at[:, other],
            dst_ref=result.at[:, tg],
            send_sem=out_send.at[step],
            recv_sem=out_recv.at[step],
            device_id=(other, me),
            device_id_type=MESH,
        )
        copy.start()
        copies.append(copy)
    own = pltpu.make_async_copy(back.at[:, tg], result.at[:, tg], local_sem.at[0])
    own.start()

    def finish(step, carry):
        outgoing(step).wait_send()
        incoming(step).wait_send()
        return carry

    lax.fori_loop(1, PLANES, finish, 0)
    own.wait()
    for copy in copies:
        copy.wait()


def apply_local(coeffs, meta, potential):
    consts = [jnp.asarray(t) for t in tables()]
    vmem = lambda *shape, dtype=F32: pltpu.VMEM(shape, dtype)
    dma = pltpu.SemaphoreType.DMA
    return pl.pallas_call(
        kernel,
        out_shape=jax.ShapeDtypeStruct((2, GROUPS, SLOT, DEPTH), F32),
        in_specs=[
            pl.BlockSpec(memory_space=pl.ANY),
            pl.BlockSpec(memory_space=pltpu.VMEM),
            pl.BlockSpec(memory_space=pl.ANY),
        ]
        + [pl.BlockSpec(memory_space=pl.ANY)] * len(consts),
        out_specs=pl.BlockSpec(memory_space=pltpu.VMEM),
        scratch_shapes=[
            vmem(2, GROUPS, SLOT, DEPTH),
            vmem(GROUPS, 8, 128),
            vmem(LAYERS, NG, NG),
        ]
        + [vmem(*t.shape, dtype=BF) for t in consts]
        + [
            vmem(PLANES, ROWS + 1, 128),
            vmem(PLANES, ROWS + 1, 128),
            vmem(2 * PLANES * ROWS, 128),
            vmem(PLANES // STEP, 2 * KEPT, STEP * 128, dtype=BF),
            vmem(2, KEPT // 2 * ROWS, KEPT),
            vmem(2, KEPT // 2 * ROWS, KEPT),
            vmem(KEPT // 2 * ROWS, 4 * KEPT, dtype=BF),
            vmem(2 * NG, LAYERS * KEPT),
            vmem(PLANES, ROWS, 128),
            vmem(PLANES, ROWS, 128),
            vmem(2, GROUPS, SLOT, DEPTH),
            dma((9,)),
            dma((GROUPS,)),
            dma((GROUPS,)),
            dma((GROUPS,)),
            dma((GROUPS,)),
            dma((GROUPS,)),
            dma((GROUPS,)),
            dma((PLANES,)),
            dma((PLANES,)),
            dma((PLANES,)),
            dma((PLANES,)),
        ],
        compiler_params=pltpu.CompilerParams(
            collective_id=0, has_side_effects=True, vmem_limit_bytes=48 * 1024 * 1024
        ),
    )(coeffs, meta, potential, *consts)


def signed(index):
    return jnp.where(index < NG // 2, index, index - NG)


def local(coeffs, potential, stick_x, stick_y, stick_count, stick_offset):
    lane = jnp.arange(128, dtype=jnp.int32)
    mine = lane // SLOT == lax.axis_index("tg")
    freq_x, freq_y = signed(stick_x), signed(stick_y)
    cell_x, cell_y = freq_x + KEPT // 2, freq_y + KEPT // 2
    ids = (cell_x // 2) * 256 + (cell_x % 2) * 128 + cell_y
    ids = jnp.where(freq_x == KEPT // 2, 0, jnp.where(freq_y == KEPT // 2, 1, ids))
    ids = jnp.where(stick_count > 0, ids, -256)
    rows = lax.broadcasted_iota(jnp.int32, (8, 128), 0)
    wide = lambda v: jnp.where(mine, jnp.tile(v, GROUPS), 0)[None]
    meta = jnp.where(
        rows == 0,
        wide(ids),
        jnp.where(rows == 1, wide(stick_count), jnp.where(rows == 2, wide(stick_offset), 0)),
    ).astype(F32)
    picked = apply_local(coeffs, meta, potential)
    depth_ids = jnp.arange(DEPTH, dtype=jnp.int32)
    live = depth_ids[None, :] < stick_count[:, None]
    z_index = (stick_offset[:, None] + depth_ids[None, :]) % NG
    squared = (freq_x**2 + freq_y**2)[:, None] + signed(z_index) ** 2
    kinetic = 0.5 * (32.0 / (NG * NG)) * squared.astype(F32)
    return jnp.where(live, picked + kinetic * coeffs, 0.0)


def solution(mesh):
    in_specs = (
        P(None, None, ("tg", "pl"), None),
        P("pl", None, None),
        P(("tg", "pl")),
        P(("tg", "pl")),
        P(("tg", "pl")),
        P(("tg", "pl")),
    )
    out_specs = P(None, None, ("tg", "pl"), None)
    return jax.shard_map(local, mesh=mesh, in_specs=in_specs, out_specs=out_specs, check_vma=False)
```

```python
import functools
import math

import jax
import jax.numpy as jnp
import numpy as np
from jax import lax
from jax.experimental import pallas as pl
from jax.experimental.pallas import tpu as pltpu
from jax.sharding import PartitionSpec as P

BF = jnp.bfloat16
F32 = jnp.float32
MESH = pl.DeviceIdType.MESH

NG = 256
DEPTH = 128
SLOT = 32
GROUPS = 4
PLANES = 64
LAYERS = 4
ROWS = 2 * LAYERS
KEPT = 128
STEP = 8


def halves(table):
    import ml_dtypes

    high = table.astype(ml_dtypes.bfloat16)
    low = (table - high.astype(np.float64)).astype(ml_dtypes.bfloat16)
    return np.stack([high, low])


def angles(rows, cols):
    return (np.multiply.outer(rows, cols) % NG) * (2.0 * math.pi / NG)


@functools.lru_cache(None)
def tables():
    angle = angles(np.arange(NG), np.arange(DEPTH)).reshape(PLANES, LAYERS, DEPTH)
    cos, sin = np.cos(angle), np.sin(angle)
    real = np.concatenate([cos, -sin], -1)
    imag = np.concatenate([sin, cos], -1)
    straight = np.concatenate([real, imag], 1).reshape(-1, 2 * DEPTH)
    turned = np.concatenate([-imag, real], 1).reshape(-1, 2 * DEPTH)
    lines = np.concatenate([straight, turned])
    angle = angles(np.arange(NG), np.arange(NG)).reshape(PLANES, LAYERS, NG)
    double = lambda t: np.concatenate([t, t], 1).reshape(-1, NG)
    phase = np.concatenate([double(np.cos(angle)), double(np.sin(angle))])
    freq = np.arange(KEPT) - KEPT // 2
    split = np.concatenate([freq[0::2], freq[1::2]])
    angle = angles(np.arange(NG), split)
    cos, sin = np.cos(angle), np.sin(angle)
    along_x = np.block([[cos, -sin], [sin, cos]])
    angle = angles(freq, np.arange(NG))
    cos, sin = np.cos(angle), np.sin(angle)
    along_y = np.block([[cos, sin], [-sin, cos]])
    scale = 1.0 / float(NG) ** 3
    return tuple(
        halves(t)
        for t in (lines, lines.T * scale, phase, along_x, along_x.T, along_y, along_y.T)
    )


def split(values):
    high = values.astype(BF)
    return high, (values - high.astype(F32)).astype(BF)


def dot(a, b):
    return jnp.dot(a, b, preferred_element_type=F32)


def dot3(a, b):
    return dot(a[0], b[0]) + (dot(a[0], b[1]) + dot(a[1], b[0]))


def settle(ref, semaphore):
    pltpu.make_async_copy(ref, ref, semaphore).wait()


def signed(index):
    return jnp.where(index < NG // 2, index, index - NG)


def quarter(index):
    index = index & 3
    one, zero = jnp.float32(1.0), jnp.float32(0.0)
    cos = jnp.where(index == 0, one, jnp.where(index == 2, -one, zero))
    sin = jnp.where(index == 1, one, jnp.where(index == 3, -one, zero))
    return cos, sin


def kernel(
    coeffs,
    potential,
    stick_x,
    stick_y,
    stick_count,
    stick_offset,
    lines_hbm,
    lines_t_hbm,
    phase_hbm,
    ax_hbm,
    axt_hbm,
    ay_hbm,
    ayt_hbm,
    result,
    group,
    coef,
    sticks,
    meta,
    metas,
    pot,
    lines,
    lines_t,
    phase,
    ax,
    axt,
    ay,
    ayt,
    send,
    recv,
    phases,
    onehot,
    spread,
    plane,
    psi,
    fields,
    sback,
    ret,
    back,
    picks,
    stick_sem,
    local_sem,
    tg_send,
    tg_recv,
    out_send,
    out_recv,
    meta_send,
    meta_recv,
    pl_send,
    pl_recv,
    rt_send,
    rt_recv,
):
    tg = lax.axis_index("tg")
    me = lax.axis_index("pl")
    fetches = [
        pltpu.make_async_copy(src, dst, local_sem.at[i])
        for i, (src, dst) in enumerate(
            [
                (coeffs.at[:, tg], group.at[:, tg]),
                (phase_hbm, phase),
                (lines_hbm, lines),
                (ax_hbm, ax),
                (ay_hbm, ay),
                (potential, pot),
                (ayt_hbm, ayt),
                (axt_hbm, axt),
                (lines_t_hbm, lines_t),
                (coeffs, coef),
            ]
        )
    ]
    rows = [
        pltpu.make_async_copy(src, sticks.at[i], stick_sem.at[i])
        for i, src in enumerate((stick_x, stick_y, stick_count, stick_offset))
    ]
    for fetch in rows + fetches[9:] + fetches[:9]:
        fetch.start()

    barrier = pltpu.get_barrier_semaphore()
    for step in range(1, GROUPS):
        pl.semaphore_signal(
            barrier, inc=1, device_id=((tg + step) & (GROUPS - 1), me), device_id_type=MESH
        )

    def greet(step, carry):
        pl.semaphore_signal(
            barrier, inc=1, device_id=(tg, (me + step) & (PLANES - 1)), device_id_type=MESH
        )
        return carry

    lax.fori_loop(1, PLANES, greet, 0, unroll=True)
    for row in rows:
        row.wait()
    mine = sticks[...]
    mine = jnp.concatenate([mine] * GROUPS, 1)
    index_x, index_y, counts, offsets = mine[0:1], mine[1:2], mine[2:3], mine[3:4]
    freq_x, freq_y = signed(index_x), signed(index_y)
    cell_x, cell_y = freq_x + KEPT // 2, freq_y + KEPT // 2
    cells = (cell_x >> 1) * 256 + (cell_x & 1) * 128 + cell_y
    cells = jnp.where(freq_x == KEPT // 2, 0, jnp.where(freq_y == KEPT // 2, 1, cells))
    cells = jnp.where(counts > 0, cells, -256)
    row_id = lax.broadcasted_iota(jnp.int32, (ROWS, 128), 0)
    own = jnp.where(row_id == 3, freq_x * freq_x + freq_y * freq_y, 0)
    own = jnp.where(row_id == 2, offsets, jnp.where(row_id == 1, counts, own))
    own = jnp.where(row_id == 0, cells, own).astype(F32)
    owner = lax.broadcasted_iota(jnp.int32, (ROWS, 128), 1) // SLOT
    meta[...] = own
    pl.semaphore_wait(barrier, GROUPS - 1 + PLANES - 1)

    fetches[9].wait()

    copies = []
    for step in (2, 1, 3):
        other = (tg + step) & (GROUPS - 1)
        for src, dst, sems in (
            (meta, metas.at[step], (meta_send, meta_recv)),
            (coef.at[:, other], group.at[:, tg], (tg_send, tg_recv)),
        ):
            copy = pltpu.make_async_remote_copy(
                src_ref=src,
                dst_ref=dst,
                send_sem=sems[0].at[step],
                recv_sem=sems[1].at[step],
                device_id=(other, me),
                device_id_type=MESH,
            )
            copy.start()
            copies.append(copy)
    for copy in copies[0::2]:
        copy.wait()
    info = own
    for step in range(1, GROUPS):
        info = jnp.where(owner == (tg - step) & (GROUPS - 1), metas[step], info)
    ids, count, offset = info[0:1], info[1:2], info[2:3]
    fetches[1].wait()
    steps = lax.broadcasted_iota(jnp.int32, (NG, 128), 0).astype(F32)
    chosen = jnp.where(steps == offset, 1.0, 0.0).astype(BF)
    phases[...] = dot(phase[0], chosen) + dot(phase[1], chosen)
    fetches[0].wait()
    fetches[2].wait()
    for copy in copies[1::2]:
        copy.wait()

    live = steps[:DEPTH] < count
    parts = []
    for part in range(2):
        rows = group[part].reshape(GROUPS * SLOT, DEPTH)
        parts.append(jnp.where(live, rows.T, 0.0))
    both = dot3((lines[0], lines[1]), split(jnp.concatenate(parts, 0)))
    moved = both[: PLANES * ROWS] * phases[: PLANES * ROWS]
    moved = moved + both[PLANES * ROWS :] * phases[PLANES * ROWS :]
    send[:, 0:ROWS, :] = moved.reshape(PLANES, ROWS, 128)
    send[:, ROWS : ROWS + 1, :] = jnp.broadcast_to(ids[None], (PLANES, 1, 128))

    def peer(ring, spot, sign):
        along_z = ((ring + 1) >> 1) * (2 * (ring & 1) - 1)
        x = ((me >> 4) + sign * (spot >> 1)) & 3
        z = ((me >> 1) + sign * along_z) & 7
        return x * 16 + z * 2 + ((me + spot) & 1)

    def outgoing(ring, spot):
        other = peer(ring, spot, 1)
        return pltpu.make_async_remote_copy(
            src_ref=send.at[other],
            dst_ref=recv.at[ring * STEP + spot],
            send_sem=pl_send.at[0],
            recv_sem=pl_recv.at[ring],
            device_id=(tg, other),
            device_id_type=MESH,
        )

    for ring in range(PLANES // STEP):
        for spot in range(0 if ring else 1, STEP):
            outgoing(ring, spot).start()
    recv[0] = send[me]

    column = lax.broadcasted_iota(jnp.int32, (2 * KEPT, 128), 0).astype(F32).astype(BF)
    second = jnp.where(lax.broadcasted_iota(jnp.int32, (16, 128), 0) >= 8, 1.0, 0.0).astype(F32)
    one, zero = jnp.ones((), BF), jnp.zeros((), BF)

    def place(g, carry):
        @pl.when(g == 0)
        def _():
            settle(recv.at[pl.ds(1, STEP - 1)], pl_recv.at[0])

        @pl.when(g > 0)
        def _():
            settle(recv.at[pl.ds(g * STEP, STEP)], pl_recv.at[g])

        block = recv[pl.ds(g * STEP, STEP)]
        left, right = [], []
        for i in range(STEP):
            high, low = split(block[i, 0:ROWS])
            row = block[i, ROWS : ROWS + 1]
            upper = jnp.floor(row * (1.0 / 256.0))
            lower = (row - 256.0 * upper).astype(BF)
            match = (upper - second).astype(BF)
            pieces = []
            for value in (high, low):
                value = jnp.concatenate([value, value], 0)
                for j in range(KEPT // 4):
                    pieces.append(jnp.where(match == jnp.asarray(2.0 * j, BF), value, zero))
            left.append(jnp.concatenate(pieces, 0))
            right.append(jnp.where(column == lower, one, zero))
        left = jnp.concatenate(left, 1)
        right = jnp.concatenate(right, 1)
        onehot[g] = right
        total = lax.dot_general(
            left, right, (((1,), (1,)), ((), ())), preferred_element_type=F32
        )
        half = KEPT // 2 * ROWS
        total = total[:half] + total[half:]

        @pl.when(g == 0)
        def _():
            spread[0] = total[:, :KEPT]
            spread[1] = total[:, KEPT:]

        @pl.when(g > 0)
        def _():
            spread[0] += total[:, :KEPT]
            spread[1] += total[:, KEPT:]

        return carry

    lax.fori_loop(0, PLANES // STEP, place, 0)

    corner = spread[0, 0:ROWS]
    lane = lax.broadcasted_iota(jnp.int32, (ROWS, 128), 1)
    edge_x = jnp.where(lane == 0, corner, 0.0).sum(axis=1, keepdims=True)
    edge_y = jnp.where(lane == 1, corner, 0.0).sum(axis=1, keepdims=True)
    spread[0, 0:ROWS] = jnp.where(lane < 2, 0.0, corner)
    fetches[3].wait()
    columns = []
    for z in range(LAYERS):
        stack = []
        for part in range(2):
            for parity in range(2):
                stack.append(spread[parity, pl.ds(part * LAYERS + z, KEPT // 2, stride=ROWS), :])
        columns.append(jnp.concatenate(stack, 0))
    mixed = dot3((ax[0], ax[1]), split(jnp.concatenate(columns, 1)))
    fields[...] = mixed

    fetches[4].wait()
    fetches[5].wait()
    fetches[6].wait()
    cos_x, sin_x = quarter(lax.broadcasted_iota(jnp.int32, (NG, KEPT), 0))
    cos_y, sin_y = quarter(lax.broadcasted_iota(jnp.int32, (1, NG), 1))
    got_x = jnp.zeros((ROWS, 128), F32)
    got_y = jnp.zeros((ROWS, 128), F32)
    centre = lax.broadcasted_iota(jnp.int32, (1, KEPT), 1) == KEPT // 2
    for z in range(LAYERS):
        re = fields[0:NG, z * KEPT : (z + 1) * KEPT]
        im = fields[NG : 2 * NG, z * KEPT : (z + 1) * KEPT]
        er = jnp.where(centre, edge_x[z : z + 1], 0.0)
        ei = jnp.where(centre, edge_x[LAYERS + z : LAYERS + z + 1], 0.0)
        re = re + (cos_x * er - sin_x * ei)
        im = im + (sin_x * er + cos_x * ei)
        wave = dot3(split(jnp.concatenate([re, im], 1)), (ay[0], ay[1]))
        er = edge_y[z : z + 1]
        ei = edge_y[LAYERS + z : LAYERS + z + 1]
        local = pot[z]
        re = (wave[:, :NG] + (cos_y * er - sin_y * ei)) * local
        im = (wave[:, NG:] + (sin_y * er + cos_y * ei)) * local
        sum_re = re.sum(axis=0, keepdims=True)
        sum_im = im.sum(axis=0, keepdims=True)
        er = (cos_y * sum_re + sin_y * sum_im).sum(axis=1, keepdims=True)
        ei = (cos_y * sum_im - sin_y * sum_re).sum(axis=1, keepdims=True)
        got_y = jnp.where(row_id == z, er, jnp.where(row_id == LAYERS + z, ei, got_y))
        mid = dot3(split(jnp.concatenate([re, im], 1)), (ayt[0], ayt[1]))
        re, im = mid[:, :KEPT], mid[:, KEPT:]
        er = (cos_x * re + sin_x * im).sum(axis=0, keepdims=True)
        ei = (cos_x * im - sin_x * re).sum(axis=0, keepdims=True)
        er = jnp.where(centre, er, 0.0).sum(axis=1, keepdims=True)
        ei = jnp.where(centre, ei, 0.0).sum(axis=1, keepdims=True)
        got_x = jnp.where(row_id == z, er, jnp.where(row_id == LAYERS + z, ei, got_x))
        fields[0:NG, z * KEPT : (z + 1) * KEPT] = re
        fields[NG : 2 * NG, z * KEPT : (z + 1) * KEPT] = im
    fetches[7].wait()
    mixed = dot3((axt[0], axt[1]), split(fields[...]))
    for z in range(LAYERS):
        for part in range(2):
            block = mixed[part * KEPT : (part + 1) * KEPT, z * KEPT : (z + 1) * KEPT]
            for parity in range(2):
                plane[parity, pl.ds(part * LAYERS + z, KEPT // 2, stride=ROWS), :] = block[
                    parity * (KEPT // 2) : (parity + 1) * (KEPT // 2)
                ]
    corner = plane[0, 0:ROWS]
    plane[0, 0:ROWS] = jnp.where(lane == 0, got_x, jnp.where(lane == 1, got_y, corner))
    for parity in range(2):
        high, low = split(plane[parity])
        psi[:, parity * KEPT : (parity + 1) * KEPT] = high
        psi[:, (2 + parity) * KEPT : (3 + parity) * KEPT] = low

    def incoming(ring, spot):
        other = peer(ring, spot, -1)
        return pltpu.make_async_remote_copy(
            src_ref=sback.at[ring * STEP + spot],
            dst_ref=ret.at[me],
            send_sem=rt_send.at[0],
            recv_sem=rt_recv.at[0],
            device_id=(tg, other),
            device_id_type=MESH,
        )

    def pick(turn, carry):
        g = PLANES // STEP - 1 - turn
        for i in range(0, STEP, 2):
            right = onehot[g, :, i * 128 : (i + 2) * 128]
            found = dot(psi[...], jnp.concatenate([right, right], 0))
            row = jnp.concatenate(
                [recv[g * STEP + i + e, ROWS : ROWS + 1] for e in range(2)], 1
            )
            upper = jnp.broadcast_to(jnp.floor(row * (1.0 / 256.0)), (ROWS, 256))
            value = jnp.zeros((ROWS, 256), F32)
            for j in range(KEPT // 2):
                value = jnp.where(upper == float(j), found[j * ROWS : (j + 1) * ROWS], value)
            for e in range(2):
                sback[g * STEP + i + e] = value[:, e * 128 : (e + 1) * 128]

        for i in range(STEP):
            if i > 0:
                incoming(g, i).start()
            else:

                @pl.when(g > 0)
                def _():
                    incoming(g, 0).start()

        return carry

    lax.fori_loop(0, PLANES // STEP, pick, 0)
    ret[me] = sback[0]

    settle(ret.at[pl.ds(1, PLANES - 1)], rt_recv.at[0])
    fetches[8].wait()
    arrived = ret[...].reshape(PLANES * ROWS, 128)
    pair = jnp.concatenate(
        [arrived * phases[: PLANES * ROWS], arrived * phases[PLANES * ROWS :]], 0
    )
    picked = dot3((lines_t[0], lines_t[1]), split(pair))
    for part in range(2):
        rows = picked[part * DEPTH : (part + 1) * DEPTH].T
        back[part] = rows.reshape(GROUPS, SLOT, DEPTH)

    copies = []
    for step in (2, 1, 3):
        other = (tg + step) & (GROUPS - 1)
        copy = pltpu.make_async_remote_copy(
            src_ref=back.at[:, other],
            dst_ref=picks.at[:, tg],
            send_sem=out_send.at[step],
            recv_sem=out_recv.at[step],
            device_id=(other, me),
            device_id_type=MESH,
        )
        copy.start()
        copies.append(copy)
    column = own.T[:SLOT]
    position = lax.broadcasted_iota(jnp.int32, (SLOT, DEPTH), 1).astype(F32)
    live = position < column[:, 1:2]
    height = position + column[:, 2:3]
    height = jnp.where(height >= float(NG), height - float(NG), height)
    height = jnp.where(height >= float(NG // 2), height - float(NG), height)
    kinetic = (0.5 * (32.0 / (NG * NG))) * (column[:, 3:4] + height * height)
    def add(band, value):
        for part in range(2):
            term = kinetic * coef[part, band]
            result[part, band] = jnp.where(live, value[part] + term, 0.0)

    add(tg, [back[0, tg], back[1, tg]])

    settle(send.at[pl.ds(1, PLANES - 1)], pl_send.at[0])
    settle(sback.at[pl.ds(1, PLANES - 1)], rt_send.at[0])
    for step, copy in zip((1, 3, 2), copies[1:] + copies[:1]):
        copy.wait()
        band = (tg - step) & (GROUPS - 1)
        add(band, [picks[0, band], picks[1, band]])


def local(coeffs, potential, stick_x, stick_y, stick_count, stick_offset):
    consts = [jnp.asarray(t) for t in tables()]
    vmem = lambda *shape, dtype=F32: pltpu.VMEM(shape, dtype)
    dma = pltpu.SemaphoreType.DMA
    args = (coeffs, potential, stick_x, stick_y, stick_count, stick_offset, *consts)
    return pl.pallas_call(
        kernel,
        out_shape=jax.ShapeDtypeStruct((2, GROUPS, SLOT, DEPTH), F32),
        in_specs=[pl.BlockSpec(memory_space=pltpu.HBM)] * len(args),
        out_specs=pl.BlockSpec(memory_space=pltpu.VMEM),
        scratch_shapes=[
            vmem(2, GROUPS, SLOT, DEPTH),
            vmem(2, GROUPS, SLOT, DEPTH),
            vmem(4, SLOT, dtype=jnp.int32),
            vmem(8, 128),
            vmem(GROUPS, 8, 128),
            vmem(LAYERS, NG, NG),
        ]
        + [vmem(*t.shape, dtype=BF) for t in consts]
        + [
            vmem(PLANES, ROWS + 1, 128),
            vmem(PLANES, ROWS + 1, 128),
            vmem(2 * PLANES * ROWS, 128),
            vmem(PLANES // STEP, 2 * KEPT, STEP * 128, dtype=BF),
            vmem(2, KEPT // 2 * ROWS, KEPT),
            vmem(2, KEPT // 2 * ROWS, KEPT),
            vmem(KEPT // 2 * ROWS, 4 * KEPT, dtype=BF),
            vmem(2 * NG, LAYERS * KEPT),
            vmem(PLANES, ROWS, 128),
            vmem(PLANES, ROWS, 128),
            vmem(2, GROUPS, SLOT, DEPTH),
            vmem(2, GROUPS, SLOT, DEPTH),
            dma((4,)),
            dma((10,)),
        ]
        + [dma((GROUPS,))] * 6
        + [dma((1,)), dma((PLANES // STEP,)), dma((1,)), dma((1,))],
        compiler_params=pltpu.CompilerParams(
            collective_id=0, has_side_effects=True, vmem_limit_bytes=62 * 1024 * 1024
        ),
    )(*args)


def solution(mesh):
    in_specs = (
        P(None, None, ("tg", "pl"), None),
        P("pl", None, None),
        P(("tg", "pl")),
        P(("tg", "pl")),
        P(("tg", "pl")),
        P(("tg", "pl")),
    )
    out_specs = P(None, None, ("tg", "pl"), None)
    return jax.shard_map(local, mesh=mesh, in_specs=in_specs, out_specs=out_specs, check_vma=False)
```

```python
import functools
import math

import jax
import jax.numpy as jnp
import numpy as np
from jax import lax
from jax.experimental import pallas as pl
from jax.experimental.pallas import tpu as pltpu
from jax.sharding import PartitionSpec as P

BF = jnp.bfloat16
F32 = jnp.float32
MESH = pl.DeviceIdType.MESH

NG = 256
DEPTH = 128
SLOT = 32
GROUPS = 4
PLANES = 64
LAYERS = 4
ROWS = 2 * LAYERS
KEPT = 128
MAIN = 20
LANES = GROUPS * MAIN + SLOT - MAIN
PART = 32
STEP = 8


def halves(table):
    import ml_dtypes

    high = table.astype(ml_dtypes.bfloat16)
    low = (table - high.astype(np.float64)).astype(ml_dtypes.bfloat16)
    return np.stack([high, low])


def angles(rows, cols):
    return (np.multiply.outer(rows, cols) % NG) * (2.0 * math.pi / NG)


@functools.lru_cache(None)
def tables():
    angle = angles(np.arange(NG), np.arange(DEPTH)).reshape(PLANES, LAYERS, DEPTH)
    cos, sin = np.cos(angle), np.sin(angle)
    real = np.concatenate([cos, -sin], -1)
    imag = np.concatenate([sin, cos], -1)
    straight = np.concatenate([real, imag], 1).reshape(-1, 2 * DEPTH)
    turned = np.concatenate([-imag, real], 1).reshape(-1, 2 * DEPTH)
    lines = np.concatenate([straight, turned])
    angle = angles(np.arange(NG), np.arange(NG)).reshape(PLANES, LAYERS, NG)
    double = lambda t: np.concatenate([t, t], 1).reshape(-1, NG)
    phase = np.concatenate([double(np.cos(angle)), double(np.sin(angle))])
    freq = np.arange(KEPT) - KEPT // 2
    split = np.concatenate([freq[0::2], freq[1::2]])
    angle = angles(np.arange(NG), split)
    cos, sin = np.cos(angle), np.sin(angle)
    along_x = np.block([[cos, -sin], [sin, cos]])
    angle = angles(freq, np.arange(NG))
    cos, sin = np.cos(angle), np.sin(angle)
    along_y = np.block([[cos, sin], [-sin, cos]])
    scale = 1.0 / float(NG) ** 3
    return tuple(
        halves(t)
        for t in (lines, lines.T * scale, phase, along_x, along_x.T, along_y, along_y.T)
    )


def split(values):
    high = values.astype(BF)
    return high, (values - high.astype(F32)).astype(BF)


def dot(a, b):
    return jnp.dot(a, b, preferred_element_type=F32)


def pack(values, chosen):
    high, low = split(values)
    return dot(high, chosen) + dot(low, chosen)


def dot3(a, b):
    return dot(
        jnp.concatenate([a[0], a[0], a[1]], 1), jnp.concatenate([b[0], b[1], b[0]], 0)
    )


def settle(ref, semaphore):
    pltpu.make_async_copy(ref, ref, semaphore).wait()


def signed(index):
    return jnp.where(index < NG // 2, index, index - NG)


def quarter(index):
    index = index & 3
    one, zero = jnp.float32(1.0), jnp.float32(0.0)
    cos = jnp.where(index == 0, one, jnp.where(index == 2, -one, zero))
    sin = jnp.where(index == 1, one, jnp.where(index == 3, -one, zero))
    return cos, sin


def kernel(
    coeffs,
    potential,
    stick_x,
    stick_y,
    stick_count,
    stick_offset,
    lines_hbm,
    lines_t_hbm,
    phase_hbm,
    ax_hbm,
    axt_hbm,
    ay_hbm,
    ayt_hbm,
    result,
    group,
    coef,
    sticks,
    meta,
    metas,
    pot,
    lines,
    lines_t,
    phase,
    ax,
    axt,
    ay,
    ayt,
    send,
    recv,
    phases,
    onehot,
    spread,
    plane,
    psi,
    fields,
    sback,
    ret,
    back,
    uppers,
    terms,
    stick_sem,
    local_sem,
    tg_send,
    tg_recv,
    out_send,
    out_recv,
    meta_send,
    meta_recv,
    pl_send,
    pl_recv,
    rt_send,
    rt_recv,
):
    tg = lax.axis_index("tg")
    me = lax.axis_index("pl")
    fetches = [
        pltpu.make_async_copy(src, dst, local_sem.at[i])
        for i, (src, dst) in enumerate(
            [
                (coeffs.at[:, tg], group.at[:, tg]),
                (phase_hbm, phase),
                (lines_hbm, lines),
                (ax_hbm, ax),
                (ay_hbm, ay),
                (potential, pot),
                (ayt_hbm, ayt),
                (axt_hbm, axt),
                (lines_t_hbm, lines_t),
                (coeffs, coef),
            ]
        )
    ]
    rows = [
        pltpu.make_async_copy(src, sticks.at[i], stick_sem.at[i])
        for i, src in enumerate((stick_x, stick_y, stick_count, stick_offset))
    ]
    for fetch in rows + fetches[9:] + fetches[:9]:
        fetch.start()

    barrier = pltpu.get_barrier_semaphore()
    for step in range(1, GROUPS):
        pl.semaphore_signal(
            barrier, inc=1, device_id=((tg + step) & (GROUPS - 1), me), device_id_type=MESH
        )

    def greet(step, carry):
        pl.semaphore_signal(
            barrier, inc=1, device_id=(tg, (me + step) & (PLANES - 1)), device_id_type=MESH
        )
        return carry

    lax.fori_loop(1, PLANES, greet, 0, unroll=True)
    for row in rows:
        row.wait()
    mine = sticks[...]
    mine = jnp.concatenate([mine] * GROUPS, 1)
    index_x, index_y, counts, offsets = mine[0:1], mine[1:2], mine[2:3], mine[3:4]
    freq_x, freq_y = signed(index_x), signed(index_y)
    cell_x, cell_y = freq_x + KEPT // 2, freq_y + KEPT // 2
    cells = (cell_x >> 1) * 256 + (cell_x & 1) * 128 + cell_y
    cells = jnp.where(freq_x == KEPT // 2, 0, jnp.where(freq_y == KEPT // 2, 1, cells))
    cells = jnp.where(counts > 0, cells + 1, 0)
    offsets = jnp.where(counts > 0, offsets, 0)
    row_id = lax.broadcasted_iota(jnp.int32, (ROWS, 128), 0)
    mine = jnp.where(row_id == 3, freq_x * freq_x + freq_y * freq_y, 0)
    mine = jnp.where(row_id == 2, offsets, jnp.where(row_id == 1, counts, mine))
    mine = jnp.where(row_id == 0, cells, mine).astype(F32)
    owner = lax.broadcasted_iota(jnp.int32, (ROWS, 128), 1) // SLOT
    meta[...] = mine
    pl.semaphore_wait(barrier, GROUPS - 1 + PLANES - 1)

    fetches[9].wait()

    def packing(slot, lane):
        spot = slot & (SLOT - 1)
        place = jnp.where(
            spot < MAIN, (slot // SLOT) * MAIN + spot, spot + (GROUPS - 1) * MAIN
        )
        return jnp.where(place == lane, 1.0, 0.0).astype(BF)

    along = lax.broadcasted_iota(jnp.int32, (128, 128), 0)
    across = lax.broadcasted_iota(jnp.int32, (128, 128), 1)
    pack_to, pack_from = packing(along, across), packing(across, along)

    copies = []
    for step in (2, 1, 3):
        other = (tg + step) & (GROUPS - 1)
        for src, dst, sems in (
            (meta, metas.at[step], (meta_send, meta_recv)),
            (coef.at[:, other], group.at[:, tg], (tg_send, tg_recv)),
        ):
            copy = pltpu.make_async_remote_copy(
                src_ref=src,
                dst_ref=dst,
                send_sem=sems[0].at[step],
                recv_sem=sems[1].at[step],
                device_id=(other, me),
                device_id_type=MESH,
            )
            copy.start()
            copies.append(copy)
    for copy in copies[0::2]:
        copy.wait()
    info = mine
    for step in range(1, GROUPS):
        info = jnp.where(owner == (tg - step) & (GROUPS - 1), metas[step], info)
    count = info[1:2]
    packed = pack(info, pack_to)
    ids, offset = packed[0:1] - 1.0, packed[2:3]
    fetches[1].wait()
    steps = lax.broadcasted_iota(jnp.int32, (NG, 128), 0).astype(F32)
    chosen = jnp.where(steps == offset, 1.0, 0.0).astype(BF)
    phases[...] = dot(phase[0], chosen) + dot(phase[1], chosen)
    fetches[0].wait()
    fetches[2].wait()
    for copy in copies[1::2]:
        copy.wait()

    live = steps[:DEPTH] < count
    parts = []
    for part in range(2):
        rows = group[part].reshape(GROUPS * SLOT, DEPTH)
        parts.append(jnp.where(live, rows.T, 0.0))
    masked = jnp.concatenate(parts, 0)
    high, low = split(masked)
    high, low = dot(high, pack_to).astype(BF), dot(low, pack_to).astype(BF)
    both = dot3((lines[0], lines[1]), (high, low))
    moved = both[: PLANES * ROWS] * phases[: PLANES * ROWS]
    moved = moved + both[PLANES * ROWS :] * phases[PLANES * ROWS :]
    send[:, 0:ROWS, :] = moved.reshape(PLANES, ROWS, 128)
    send[:, ROWS : ROWS + 1, :] = jnp.broadcast_to(ids[None], (PLANES, 1, 128))

    def peer(ring, spot, sign):
        along_z = ((ring + 1) >> 1) * (2 * (ring & 1) - 1)
        x = ((me >> 4) + sign * (spot >> 1)) & 3
        z = ((me >> 1) + sign * along_z) & 7
        return x * 16 + z * 2 + ((me + spot) & 1)

    def outgoing(ring, spot):
        other = peer(ring, spot, 1)
        return pltpu.make_async_remote_copy(
            src_ref=send.at[other],
            dst_ref=recv.at[ring * STEP + spot],
            send_sem=pl_send.at[0],
            recv_sem=pl_recv.at[ring],
            device_id=(tg, other),
            device_id_type=MESH,
        )

    for ring in range(PLANES // STEP):
        for spot in range(0 if ring else 1, STEP):
            outgoing(ring, spot).start()
    recv[0] = send[me]

    height = steps[:DEPTH] + info[2:3]
    height = jnp.where(height >= float(NG), height - float(NG), height)
    height = jnp.where(height >= float(NG // 2), height - float(NG), height)
    kinetic = (0.5 * (32.0 / (NG * NG))) * (info[3:4] + height * height)
    terms[...] = jnp.concatenate([kinetic, kinetic], 0) * masked

    column = lax.broadcasted_iota(jnp.int32, (2 * KEPT, 128), 0).astype(F32).astype(BF)
    second = jnp.where(lax.broadcasted_iota(jnp.int32, (16, 128), 0) >= 8, 1.0, 0.0).astype(F32)
    one, zero = jnp.ones((), BF), jnp.zeros((), BF)

    lane9 = lax.broadcasted_iota(jnp.int32, (ROWS + 1, 128), 1)

    def place(g, carry):
        @pl.when(g == 0)
        def _():
            settle(recv.at[pl.ds(1, STEP - 1)], pl_recv.at[0])

        @pl.when(g > 0)
        def _():
            settle(recv.at[pl.ds(g * STEP, STEP)], pl_recv.at[g])

        block = recv[pl.ds(g * STEP, STEP)]
        left, right = [], []
        tiles = []
        for i in range(0, STEP, 4):
            for t in range(3):
                spread_out = pltpu.roll(block[i + 3], 96 - PART * t, 1)
                tiles.append(jnp.where(lane9 < 96, block[i + t], spread_out))
        for i, tile in enumerate(tiles):
            high, low = split(tile[0:ROWS])
            row = tile[ROWS : ROWS + 1]
            upper = jnp.floor(row * (1.0 / 256.0))
            lower = (row - 256.0 * upper).astype(BF)
            uppers[g * len(tiles) + i] = jnp.broadcast_to(upper, (ROWS, 128))
            match = (upper - second).astype(BF)
            pieces = []
            for value in (high, low):
                value = jnp.concatenate([value, value], 0)
                for j in range(KEPT // 4):
                    pieces.append(jnp.where(match == jnp.asarray(2.0 * j, BF), value, zero))
            left.append(jnp.concatenate(pieces, 0))
            right.append(jnp.where(column == lower, one, zero))
        left = jnp.concatenate(left, 1)
        right = jnp.concatenate(right, 1)
        onehot[g] = right
        total = lax.dot_general(
            left, right, (((1,), (1,)), ((), ())), preferred_element_type=F32
        )
        half = KEPT // 2 * ROWS
        total = total[:half] + total[half:]

        @pl.when(g == 0)
        def _():
            spread[0] = total[:, :KEPT]
            spread[1] = total[:, KEPT:]

        @pl.when(g > 0)
        def _():
            spread[0] += total[:, :KEPT]
            spread[1] += total[:, KEPT:]

        return carry

    lax.fori_loop(0, PLANES // STEP, place, 0)

    corner = spread[0, 0:ROWS]
    lane = lax.broadcasted_iota(jnp.int32, (ROWS, 128), 1)
    edge_x = jnp.where(lane == 0, corner, 0.0).sum(axis=1, keepdims=True)
    edge_y = jnp.where(lane == 1, corner, 0.0).sum(axis=1, keepdims=True)
    spread[0, 0:ROWS] = jnp.where(lane < 2, 0.0, corner)
    fetches[3].wait()
    columns = []
    for z in range(LAYERS):
        stack = []
        for part in range(2):
            for parity in range(2):
                stack.append(spread[parity, pl.ds(part * LAYERS + z, KEPT // 2, stride=ROWS), :])
        columns.append(jnp.concatenate(stack, 0))
    mixed = dot3((ax[0], ax[1]), split(jnp.concatenate(columns, 1)))
    fields[...] = mixed

    fetches[4].wait()
    fetches[5].wait()
    fetches[6].wait()
    cos_x, sin_x = quarter(lax.broadcasted_iota(jnp.int32, (NG, KEPT), 0))
    cos_y, sin_y = quarter(lax.broadcasted_iota(jnp.int32, (1, NG), 1))
    got_x = jnp.zeros((ROWS, 128), F32)
    got_y = jnp.zeros((ROWS, 128), F32)
    centre = lax.broadcasted_iota(jnp.int32, (1, KEPT), 1) == KEPT // 2
    for z in range(LAYERS):
        re = fields[0:NG, z * KEPT : (z + 1) * KEPT]
        im = fields[NG : 2 * NG, z * KEPT : (z + 1) * KEPT]
        er = jnp.where(centre, edge_x[z : z + 1], 0.0)
        ei = jnp.where(centre, edge_x[LAYERS + z : LAYERS + z + 1], 0.0)
        re = re + (cos_x * er - sin_x * ei)
        im = im + (sin_x * er + cos_x * ei)
        wave = dot3(split(jnp.concatenate([re, im], 1)), (ay[0], ay[1]))
        er = edge_y[z : z + 1]
        ei = edge_y[LAYERS + z : LAYERS + z + 1]
        local = pot[z]
        re = (wave[:, :NG] + (cos_y * er - sin_y * ei)) * local
        im = (wave[:, NG:] + (sin_y * er + cos_y * ei)) * local
        sum_re = re.sum(axis=0, keepdims=True)
        sum_im = im.sum(axis=0, keepdims=True)
        er = (cos_y * sum_re + sin_y * sum_im).sum(axis=1, keepdims=True)
        ei = (cos_y * sum_im - sin_y * sum_re).sum(axis=1, keepdims=True)
        got_y = jnp.where(row_id == z, er, jnp.where(row_id == LAYERS + z, ei, got_y))
        mid = dot3(split(jnp.concatenate([re, im], 1)), (ayt[0], ayt[1]))
        re, im = mid[:, :KEPT], mid[:, KEPT:]
        er = (cos_x * re + sin_x * im).sum(axis=0, keepdims=True)
        ei = (cos_x * im - sin_x * re).sum(axis=0, keepdims=True)
        er = jnp.where(centre, er, 0.0).sum(axis=1, keepdims=True)
        ei = jnp.where(centre, ei, 0.0).sum(axis=1, keepdims=True)
        got_x = jnp.where(row_id == z, er, jnp.where(row_id == LAYERS + z, ei, got_x))
        fields[0:NG, z * KEPT : (z + 1) * KEPT] = re
        fields[NG : 2 * NG, z * KEPT : (z + 1) * KEPT] = im
    fetches[7].wait()
    mixed = dot3((axt[0], axt[1]), split(fields[...]))
    for z in range(LAYERS):
        for part in range(2):
            block = mixed[part * KEPT : (part + 1) * KEPT, z * KEPT : (z + 1) * KEPT]
            for parity in range(2):
                plane[parity, pl.ds(part * LAYERS + z, KEPT // 2, stride=ROWS), :] = block[
                    parity * (KEPT // 2) : (parity + 1) * (KEPT // 2)
                ]
    corner = plane[0, 0:ROWS]
    plane[0, 0:ROWS] = jnp.where(lane == 0, got_x, jnp.where(lane == 1, got_y, corner))
    for parity in range(2):
        high, low = split(plane[parity])
        psi[:, parity * KEPT : (parity + 1) * KEPT] = high
        psi[:, (2 + parity) * KEPT : (3 + parity) * KEPT] = low

    def incoming(ring, spot):
        other = peer(ring, spot, -1)
        return pltpu.make_async_remote_copy(
            src_ref=sback.at[ring * STEP + spot],
            dst_ref=ret.at[me],
            send_sem=rt_send.at[0],
            recv_sem=rt_recv.at[0],
            device_id=(tg, other),
            device_id_type=MESH,
        )

    def pick(turn, carry):
        g = PLANES // STEP - 1 - turn
        tiles = []
        for i in range(0, STEP * 3 // 4, 2):
            right = onehot[g, :, i * 128 : (i + 2) * 128]
            found = dot(psi[...], jnp.concatenate([right, right], 0))
            upper = jnp.concatenate(
                [uppers[g * (STEP * 3 // 4) + i + e] for e in range(2)], 1
            )
            value = jnp.zeros((ROWS, 256), F32)
            for j in range(KEPT // 2):
                value = jnp.where(upper == float(j), found[j * ROWS : (j + 1) * ROWS], value)
            tiles += [value[:, :128], value[:, 128:]]
        for i in range(0, STEP, 4):
            three = tiles[i * 3 // 4 : i * 3 // 4 + 3]
            for t in range(3):
                sback[g * STEP + i + t] = three[t]
            turned = [pltpu.roll(three[t], PART * (t + 1), 1) for t in range(3)]
            sback[g * STEP + i + 3] = jnp.where(
                lane < PART, turned[0], jnp.where(lane < 2 * PART, turned[1], turned[2])
            )
        for i in range(STEP):
            if i > 0:
                incoming(g, i).start()
            else:

                @pl.when(g > 0)
                def _():
                    incoming(g, 0).start()

        return carry

    lax.fori_loop(0, PLANES // STEP, pick, 0)
    ret[me] = sback[0]

    settle(ret.at[pl.ds(1, PLANES - 1)], rt_recv.at[0])
    fetches[8].wait()
    arrived = ret[...].reshape(PLANES * ROWS, 128)
    pair = jnp.concatenate(
        [arrived * phases[: PLANES * ROWS], arrived * phases[PLANES * ROWS :]], 0
    )
    picked = pack(dot3((lines_t[0], lines_t[1]), split(pair)), pack_from) + terms[...]
    picked = jnp.where(jnp.concatenate([live, live], 0), picked, 0.0)
    for part in range(2):
        rows = picked[part * DEPTH : (part + 1) * DEPTH].T
        back[part] = rows.reshape(GROUPS, SLOT, DEPTH)

    copies = []
    for step in (2, 1, 3):
        other = (tg + step) & (GROUPS - 1)
        copy = pltpu.make_async_remote_copy(
            src_ref=back.at[:, other],
            dst_ref=result.at[:, tg],
            send_sem=out_send.at[step],
            recv_sem=out_recv.at[step],
            device_id=(other, me),
            device_id_type=MESH,
        )
        copy.start()
        copies.append(copy)
    own = pltpu.make_async_copy(back.at[:, tg], result.at[:, tg], stick_sem.at[0])
    own.start()
    settle(send.at[pl.ds(1, PLANES - 1)], pl_send.at[0])
    settle(sback.at[pl.ds(1, PLANES - 1)], rt_send.at[0])
    own.wait()
    for copy in copies:
        copy.wait()


def local(coeffs, potential, stick_x, stick_y, stick_count, stick_offset):
    consts = [jnp.asarray(t) for t in tables()]
    vmem = lambda *shape, dtype=F32: pltpu.VMEM(shape, dtype)
    dma = pltpu.SemaphoreType.DMA
    args = (coeffs, potential, stick_x, stick_y, stick_count, stick_offset, *consts)
    return pl.pallas_call(
        kernel,
        out_shape=jax.ShapeDtypeStruct((2, GROUPS, SLOT, DEPTH), F32),
        in_specs=[pl.BlockSpec(memory_space=pltpu.HBM)] * len(args),
        out_specs=pl.BlockSpec(memory_space=pltpu.HBM),
        scratch_shapes=[
            vmem(2, GROUPS, SLOT, DEPTH),
            vmem(2, GROUPS, SLOT, DEPTH),
            vmem(4, SLOT, dtype=jnp.int32),
            vmem(8, 128),
            vmem(GROUPS, 8, 128),
            vmem(LAYERS, NG, NG),
        ]
        + [vmem(*t.shape, dtype=BF) for t in consts]
        + [
            vmem(PLANES, ROWS + 1, 128),
            vmem(PLANES, ROWS + 1, 128),
            vmem(2 * PLANES * ROWS, 128),
            vmem(PLANES // STEP, 2 * KEPT, STEP * 96, dtype=BF),
            vmem(2, KEPT // 2 * ROWS, KEPT),
            vmem(2, KEPT // 2 * ROWS, KEPT),
            vmem(KEPT // 2 * ROWS, 4 * KEPT, dtype=BF),
            vmem(2 * NG, LAYERS * KEPT),
            vmem(PLANES, ROWS, 128),
            vmem(PLANES, ROWS, 128),
            vmem(2, GROUPS, SLOT, DEPTH),
            vmem(PLANES * 3 // 4, ROWS, 128),
            vmem(2 * DEPTH, 128),
            dma((4,)),
            dma((10,)),
        ]
        + [dma((GROUPS,))] * 6
        + [dma((1,)), dma((PLANES // STEP,)), dma((1,)), dma((1,))],
        compiler_params=pltpu.CompilerParams(
            collective_id=0, has_side_effects=True, vmem_limit_bytes=62 * 1024 * 1024
        ),
    )(*args)


def solution(mesh):
    in_specs = (
        P(None, None, ("tg", "pl"), None),
        P("pl", None, None),
        P(("tg", "pl")),
        P(("tg", "pl")),
        P(("tg", "pl")),
        P(("tg", "pl")),
    )
    out_specs = P(None, None, ("tg", "pl"), None)
    return jax.shard_map(local, mesh=mesh, in_specs=in_specs, out_specs=out_specs, check_vma=False)
```

```python
import functools
import math

import jax
import jax.numpy as jnp
import numpy as np
from jax import lax
from jax.experimental import pallas as pl
from jax.experimental.pallas import tpu as pltpu
from jax.sharding import PartitionSpec as P

BF = jnp.bfloat16
F32 = jnp.float32
MESH = pl.DeviceIdType.MESH

NG = 256
DEPTH = 128
SLOT = 32
GROUPS = 4
PLANES = 64
LAYERS = 4
ROWS = 2 * LAYERS
KEPT = 128
MAIN = 20
WIRE = 6
STEP = 8


def halves(table):
    import ml_dtypes

    high = table.astype(ml_dtypes.bfloat16)
    low = (table - high.astype(np.float64)).astype(ml_dtypes.bfloat16)
    return np.stack([high, low])


def angles(rows, cols):
    return (np.multiply.outer(rows, cols) % NG) * (2.0 * math.pi / NG)


@functools.lru_cache(None)
def tables():
    planes = np.add.outer(np.arange(LAYERS), LAYERS * np.arange(PLANES)).reshape(-1)
    angle = angles(planes, np.arange(DEPTH))
    cos, sin = np.cos(angle), np.sin(angle)
    lines = np.block([[cos, -sin], [sin, cos]])
    angle = angles(planes, np.arange(NG))
    phase = np.concatenate([np.cos(angle), np.sin(angle)])
    freq = np.arange(KEPT) - KEPT // 2
    split = np.concatenate([freq[0::2], freq[1::2]])
    angle = angles(np.arange(NG), split)
    cos, sin = np.cos(angle), np.sin(angle)
    along_x = np.block([[cos, -sin], [sin, cos]])
    angle = angles(freq, np.arange(NG))
    cos, sin = np.cos(angle), np.sin(angle)
    along_y = np.block([[cos, sin], [-sin, cos]])
    scale = 1.0 / float(NG) ** 3
    return tuple(
        halves(t)
        for t in (lines, lines.T * scale, phase, along_x, along_x.T, along_y, along_y.T)
    )


def split(values):
    high = values.astype(BF)
    return high, (values - high.astype(F32)).astype(BF)


def dot(a, b):
    return jnp.dot(a, b, preferred_element_type=F32)


def pack(values, chosen):
    high, low = split(values)
    return dot(high, chosen) + dot(low, chosen)


def dot3(a, b):
    return dot(
        jnp.concatenate([a[0], a[0], a[1]], 1), jnp.concatenate([b[0], b[1], b[0]], 0)
    )


def settle(ref, semaphore):
    pltpu.make_async_copy(ref, ref, semaphore).wait()


def signed(index):
    return jnp.where(index < NG // 2, index, index - NG)


def quarter(index):
    index = index & 3
    one, zero = jnp.float32(1.0), jnp.float32(0.0)
    cos = jnp.where(index == 0, one, jnp.where(index == 2, -one, zero))
    sin = jnp.where(index == 1, one, jnp.where(index == 3, -one, zero))
    return cos, sin


def kernel(
    coeffs,
    potential,
    stick_x,
    stick_y,
    stick_count,
    stick_offset,
    lines_hbm,
    lines_t_hbm,
    phase_hbm,
    ax_hbm,
    axt_hbm,
    ay_hbm,
    ayt_hbm,
    result,
    group,
    coef,
    sticks,
    meta,
    metas,
    pot,
    lines,
    lines_t,
    phase,
    ax,
    axt,
    ay,
    ayt,
    send,
    recv,
    phase_a,
    phase_b,
    names,
    idents,
    onehot,
    spread,
    plane,
    psi,
    fields,
    sback,
    ret,
    back,
    uppers,
    terms,
    stick_sem,
    local_sem,
    id_send,
    id_recv,
    tg_send,
    tg_recv,
    out_send,
    out_recv,
    meta_send,
    meta_recv,
    pl_send,
    pl_recv,
    rt_send,
    rt_recv,
):
    tg = lax.axis_index("tg")
    me = lax.axis_index("pl")
    fetches = [
        pltpu.make_async_copy(src, dst, local_sem.at[i])
        for i, (src, dst) in enumerate(
            [
                (coeffs.at[:, tg], group.at[:, tg]),
                (phase_hbm, phase),
                (lines_hbm, lines),
                (ax_hbm, ax),
                (ay_hbm, ay),
                (potential, pot),
                (ayt_hbm, ayt),
                (axt_hbm, axt),
                (lines_t_hbm, lines_t),
                (coeffs, coef),
            ]
        )
    ]
    rows = [
        pltpu.make_async_copy(src, sticks.at[i], stick_sem.at[i])
        for i, src in enumerate((stick_x, stick_y, stick_count, stick_offset))
    ]
    for fetch in rows + fetches[9:] + fetches[:9]:
        fetch.start()

    barrier = pltpu.get_barrier_semaphore()
    for step in range(1, GROUPS):
        pl.semaphore_signal(
            barrier, inc=1, device_id=((tg + step) & (GROUPS - 1), me), device_id_type=MESH
        )

    def greet(step, carry):
        pl.semaphore_signal(
            barrier, inc=1, device_id=(tg, (me + step) & (PLANES - 1)), device_id_type=MESH
        )
        return carry

    lax.fori_loop(1, PLANES, greet, 0, unroll=True)
    for row in rows:
        row.wait()
    mine = sticks[...]
    mine = jnp.concatenate([mine] * GROUPS, 1)
    index_x, index_y, counts, offsets = mine[0:1], mine[1:2], mine[2:3], mine[3:4]
    freq_x, freq_y = signed(index_x), signed(index_y)
    cell_x, cell_y = freq_x + KEPT // 2, freq_y + KEPT // 2
    cells = (cell_x >> 1) * 256 + (cell_x & 1) * 128 + cell_y
    cells = jnp.where(freq_x == KEPT // 2, 0, jnp.where(freq_y == KEPT // 2, 1, cells))
    cells = jnp.where(counts > 0, cells + 1, 0)
    offsets = jnp.where(counts > 0, offsets, 0)
    row_id = lax.broadcasted_iota(jnp.int32, (ROWS, 128), 0)
    mine = jnp.where(row_id == 3, freq_x * freq_x + freq_y * freq_y, 0)
    mine = jnp.where(row_id == 2, offsets, jnp.where(row_id == 1, counts, mine))
    mine = jnp.where(row_id == 0, cells, mine).astype(F32)
    owner = lax.broadcasted_iota(jnp.int32, (ROWS, 128), 1) // SLOT
    meta[...] = mine
    pl.semaphore_wait(barrier, GROUPS - 1 + PLANES - 1)

    fetches[9].wait()

    def packing(slot, place):
        spot = slot & (SLOT - 1)
        own = jnp.where(spot < MAIN, (slot // SLOT) * MAIN + spot, spot + (GROUPS - 1) * MAIN)
        return jnp.where(own == place, 1.0, 0.0).astype(BF)

    along = lax.broadcasted_iota(jnp.int32, (128, 128), 0)
    across = lax.broadcasted_iota(jnp.int32, (128, 128), 1)
    pack_to = jnp.concatenate(
        [packing(along, across & 63), packing(along, 64 + (across & 31))], 1
    )
    pack_from = packing(across, along)
    lane = lax.broadcasted_iota(jnp.int32, (ROWS, 128), 1)
    sub = lax.broadcasted_iota(jnp.int32, (ROWS, 128), 0)
    half = lane < 64
    half1, quad1 = half[0:1], lane[0:1] // 32
    quad = lane // 32
    sign = jnp.where(half1, 1.0, -1.0)
    swap = lambda v: pltpu.roll(v, 64, 1)

    layer = sub & (LAYERS - 1)

    def by_layer(values):
        low = jnp.where(layer == 0, values[0], values[1])
        return jnp.where(layer < 2, low, jnp.where(layer == 2, values[2], values[3]))

    def diagonal(rows):
        out = rows[0:PLANES]
        for b in range(1, LAYERS):
            out = jnp.where(quad1 == b, rows[b * PLANES : (b + 1) * PLANES], out)
        return out

    copies = []
    for step in (2, 1, 3):
        other = (tg + step) & (GROUPS - 1)
        for src, dst, sems in (
            (meta, metas.at[step], (meta_send, meta_recv)),
            (coef.at[:, other], group.at[:, tg], (tg_send, tg_recv)),
        ):
            copy = pltpu.make_async_remote_copy(
                src_ref=src,
                dst_ref=dst,
                send_sem=sems[0].at[step],
                recv_sem=sems[1].at[step],
                device_id=(other, me),
                device_id_type=MESH,
            )
            copy.start()
            copies.append(copy)
    for copy in copies[0::2]:
        copy.wait()
    info = mine
    for step in range(1, GROUPS):
        info = jnp.where(owner == (tg - step) & (GROUPS - 1), metas[step], info)
    count = info[1:2]
    packed = pack(info, pack_to)
    ids, offset = packed[0:1] - 1.0, packed[2:3]
    names[0] = jnp.where(half1, ids[:, 0:128], ids[:, 128:256])

    def peer(ring, spot, sign):
        along_z = ((ring + 1) >> 1) * (2 * (ring & 1) - 1)
        x = ((me >> 4) + sign * (spot >> 1)) & 3
        z = ((me >> 1) + sign * along_z) & 7
        return x * 16 + z * 2 + ((me + spot) & 1)

    def introduce(ring, spot):
        return pltpu.make_async_remote_copy(
            src_ref=names.at[0],
            dst_ref=idents.at[ring * STEP + spot],
            send_sem=id_send.at[0],
            recv_sem=id_recv.at[0],
            device_id=(tg, peer(ring, spot, 1)),
            device_id_type=MESH,
        )

    for ring in range(PLANES // STEP):
        for spot in range(0 if ring else 1, STEP):
            introduce(ring, spot).start()
    idents[0] = names[0]
    fetches[1].wait()
    steps = lax.broadcasted_iota(jnp.int32, (NG, 128), 0).astype(F32)
    chosen = jnp.concatenate(
        [jnp.where(steps == offset[:, t * 128 : (t + 1) * 128], 1.0, 0.0) for t in range(2)], 1
    ).astype(BF)
    turns = dot(phase[0], chosen) + dot(phase[1], chosen)
    phase_a[...] = turns[:, :128]
    for trig in range(2):
        phase_b[trig] = diagonal(turns[trig * NG : (trig + 1) * NG, 128:])
    fetches[0].wait()
    fetches[2].wait()
    for copy in copies[1::2]:
        copy.wait()

    live = steps[:DEPTH] < count
    parts = []
    for part in range(2):
        rows = group[part].reshape(GROUPS * SLOT, DEPTH)
        parts.append(jnp.where(live, rows.T, 0.0))
    masked = jnp.concatenate(parts, 0)
    sides = []
    for value in split(masked):
        value = dot(value, pack_to)
        re, im = value[:DEPTH, :128], value[DEPTH:, :128]
        left = jnp.concatenate([jnp.where(half1, re, im), jnp.where(half1, im, -re)], 0)
        sides.append(jnp.concatenate([left, value[:, 128:]], 1).astype(BF))
    both = dot3((lines[0], lines[1]), sides)
    moved = both[:NG, :128] * phase_a[:NG] - both[NG:, :128] * phase_a[NG:]
    for z in range(LAYERS):
        send[pl.ds(z, PLANES, stride=ROWS), :] = moved[z * PLANES : (z + 1) * PLANES]
    re, im = diagonal(both[:NG, 128:]), diagonal(both[NG:, 128:])
    send[pl.ds(LAYERS, PLANES, stride=ROWS), :] = re * phase_b[0] - im * phase_b[1]
    send[pl.ds(LAYERS + 1, PLANES, stride=ROWS), :] = im * phase_b[0] + re * phase_b[1]

    def spot_rows(index, rows):
        return pl.ds(pl.multiple_of(index * ROWS, ROWS), rows)

    def outgoing(ring, spot):
        other = peer(ring, spot, 1)
        return pltpu.make_async_remote_copy(
            src_ref=send.at[spot_rows(other, WIRE)],
            dst_ref=recv.at[spot_rows(ring * STEP + spot, WIRE)],
            send_sem=pl_send.at[0],
            recv_sem=pl_recv.at[ring],
            device_id=(tg, other),
            device_id_type=MESH,
        )

    for ring in range(PLANES // STEP):
        for spot in range(0 if ring else 1, STEP):
            outgoing(ring, spot).start()
    recv[0:ROWS] = send[spot_rows(me, ROWS)]

    height = steps[:DEPTH] + info[2:3]
    height = jnp.where(height >= float(NG), height - float(NG), height)
    height = jnp.where(height >= float(NG // 2), height - float(NG), height)
    kinetic = (0.5 * (32.0 / (NG * NG))) * (info[3:4] + height * height)
    terms[...] = jnp.concatenate([kinetic, kinetic], 0) * masked

    column = lax.broadcasted_iota(jnp.int32, (2 * KEPT, 128), 0).astype(F32).astype(BF)
    second = jnp.where(lax.broadcasted_iota(jnp.int32, (16, 128), 0) >= 8, 1.0, 0.0).astype(F32)
    one, zero = jnp.ones((), BF), jnp.zeros((), BF)

    settle(idents.at[pl.ds(1, PLANES - 1)], id_recv.at[0])

    def place(g, carry):
        @pl.when(g == 0)
        def _():
            settle(recv.at[pl.ds(0, (STEP - 1) * WIRE)], pl_recv.at[0])

        @pl.when(g > 0)
        def _():
            settle(recv.at[pl.ds(0, STEP * WIRE)], pl_recv.at[g])

        block = recv[spot_rows(g * STEP, STEP * ROWS)]
        names8 = idents[pl.ds(g * STEP, STEP)]
        left, right = [], []
        tiles = []
        for i in range(0, STEP, 4):
            rows = [block[(i + j) * ROWS : (i + j + 1) * ROWS] for j in range(4)]
            ids8 = [jnp.broadcast_to(names8[i + j], (ROWS, 128)) for j in range(4)]
            for a in (0, 2):
                top = jnp.where(half, rows[a], swap(rows[a + 1]))
                low = jnp.where(half, swap(rows[a]), rows[a + 1])
                tile = jnp.where(sub < LAYERS, top, pltpu.roll(low, LAYERS, 0))
                tiles.append((tile, jnp.where(half, ids8[a], swap(ids8[a + 1]))))
            wide = [
                jnp.where(sub < LAYERS, row[LAYERS : LAYERS + 1], row[LAYERS + 1 : LAYERS + 2])
                for row in rows
            ]
            name = jnp.zeros((ROWS, 128), F32)
            for j in range(4):
                near = ids8[j] if j == 2 else pltpu.roll(ids8[j], (32 * j - 64) % 128, 1)
                name = jnp.where(quad == j, near, name)
            tile = by_layer(wide)
            for d in range(1, 4):
                shifted = pltpu.roll(by_layer(wide[d:] + wide[:d]), 32 * d, 1)
                tile = jnp.where(quad == (layer + d) & 3, shifted, tile)
            tiles.append((tile, name))
        for i, (tile, name) in enumerate(tiles):
            high, low = split(tile)
            upper = jnp.floor(name * (1.0 / 256.0))
            lower = (name - 256.0 * upper)[0:1].astype(BF)
            uppers[g * len(tiles) + i] = upper
            upper = jnp.concatenate([upper, upper], 0)
            match = (upper - second).astype(BF)
            pieces = []
            for value in (high, low):
                value = jnp.concatenate([value, value], 0)
                for j in range(KEPT // 4):
                    pieces.append(jnp.where(match == jnp.asarray(2.0 * j, BF), value, zero))
            left.append(jnp.concatenate(pieces, 0))
            right.append(jnp.where(column == lower, one, zero))
        left = jnp.concatenate(left, 1)
        right = jnp.concatenate(right, 1)
        onehot[g] = right
        total = lax.dot_general(
            left, right, (((1,), (1,)), ((), ())), preferred_element_type=F32
        )
        total = total[: KEPT // 2 * ROWS] + total[KEPT // 2 * ROWS :]

        @pl.when(g == 0)
        def _():
            spread[0] = total[:, :KEPT]
            spread[1] = total[:, KEPT:]

        @pl.when(g > 0)
        def _():
            spread[0] += total[:, :KEPT]
            spread[1] += total[:, KEPT:]

        return carry

    lax.fori_loop(0, PLANES // STEP, place, 0)

    corner = spread[0, 0:ROWS]
    edge_x = jnp.where(lane == 0, corner, 0.0).sum(axis=1, keepdims=True)
    edge_y = jnp.where(lane == 1, corner, 0.0).sum(axis=1, keepdims=True)
    spread[0, 0:ROWS] = jnp.where(lane < 2, 0.0, corner)
    fetches[3].wait()
    columns = []
    for z in range(LAYERS):
        stack = []
        for part in range(2):
            for parity in range(2):
                stack.append(spread[parity, pl.ds(part * LAYERS + z, KEPT // 2, stride=ROWS), :])
        columns.append(jnp.concatenate(stack, 0))
    mixed = dot3((ax[0], ax[1]), split(jnp.concatenate(columns, 1)))
    fields[...] = mixed

    fetches[4].wait()
    fetches[5].wait()
    fetches[6].wait()
    cos_x, sin_x = quarter(lax.broadcasted_iota(jnp.int32, (NG, KEPT), 0))
    cos_y, sin_y = quarter(lax.broadcasted_iota(jnp.int32, (1, NG), 1))
    got_x = jnp.zeros((ROWS, 128), F32)
    got_y = jnp.zeros((ROWS, 128), F32)
    centre = lax.broadcasted_iota(jnp.int32, (1, KEPT), 1) == KEPT // 2
    for z in range(LAYERS):
        re = fields[0:NG, z * KEPT : (z + 1) * KEPT]
        im = fields[NG : 2 * NG, z * KEPT : (z + 1) * KEPT]
        er = jnp.where(centre, edge_x[z : z + 1], 0.0)
        ei = jnp.where(centre, edge_x[LAYERS + z : LAYERS + z + 1], 0.0)
        re = re + (cos_x * er - sin_x * ei)
        im = im + (sin_x * er + cos_x * ei)
        wave = dot3(split(jnp.concatenate([re, im], 1)), (ay[0], ay[1]))
        er = edge_y[z : z + 1]
        ei = edge_y[LAYERS + z : LAYERS + z + 1]
        local = pot[z]
        re = (wave[:, :NG] + (cos_y * er - sin_y * ei)) * local
        im = (wave[:, NG:] + (sin_y * er + cos_y * ei)) * local
        sum_re = re.sum(axis=0, keepdims=True)
        sum_im = im.sum(axis=0, keepdims=True)
        er = (cos_y * sum_re + sin_y * sum_im).sum(axis=1, keepdims=True)
        ei = (cos_y * sum_im - sin_y * sum_re).sum(axis=1, keepdims=True)
        got_y = jnp.where(row_id == z, er, jnp.where(row_id == LAYERS + z, ei, got_y))
        mid = dot3(split(jnp.concatenate([re, im], 1)), (ayt[0], ayt[1]))
        re, im = mid[:, :KEPT], mid[:, KEPT:]
        er = (cos_x * re + sin_x * im).sum(axis=0, keepdims=True)
        ei = (cos_x * im - sin_x * re).sum(axis=0, keepdims=True)
        er = jnp.where(centre, er, 0.0).sum(axis=1, keepdims=True)
        ei = jnp.where(centre, ei, 0.0).sum(axis=1, keepdims=True)
        got_x = jnp.where(row_id == z, er, jnp.where(row_id == LAYERS + z, ei, got_x))
        fields[0:NG, z * KEPT : (z + 1) * KEPT] = re
        fields[NG : 2 * NG, z * KEPT : (z + 1) * KEPT] = im
    fetches[7].wait()
    mixed = dot3((axt[0], axt[1]), split(fields[...]))
    for z in range(LAYERS):
        for part in range(2):
            block = mixed[part * KEPT : (part + 1) * KEPT, z * KEPT : (z + 1) * KEPT]
            for parity in range(2):
                plane[parity, pl.ds(part * LAYERS + z, KEPT // 2, stride=ROWS), :] = block[
                    parity * (KEPT // 2) : (parity + 1) * (KEPT // 2)
                ]
    corner = plane[0, 0:ROWS]
    plane[0, 0:ROWS] = jnp.where(lane == 0, got_x, jnp.where(lane == 1, got_y, corner))
    for parity in range(2):
        high, low = split(plane[parity])
        psi[:, parity * KEPT : (parity + 1) * KEPT] = high
        psi[:, (2 + parity) * KEPT : (3 + parity) * KEPT] = low

    def incoming(ring, spot):
        other = peer(ring, spot, -1)
        return pltpu.make_async_remote_copy(
            src_ref=sback.at[spot_rows(ring * STEP + spot, WIRE)],
            dst_ref=ret.at[spot_rows(me, WIRE)],
            send_sem=rt_send.at[0],
            recv_sem=rt_recv.at[0],
            device_id=(tg, other),
            device_id_type=MESH,
        )

    def pick(turn, carry):
        g = PLANES // STEP - 1 - turn
        tiles = []
        for i in range(0, STEP * 3 // 4, 2):
            right = onehot[g, :, i * 128 : (i + 2) * 128]
            found = dot(psi[...], jnp.concatenate([right, right], 0))
            upper = jnp.concatenate(
                [uppers[g * (STEP * 3 // 4) + i + e] for e in range(2)], 1
            )
            value = jnp.zeros((ROWS, 256), F32)
            for j in range(KEPT // 2):
                value = jnp.where(upper == float(j), found[j * ROWS : (j + 1) * ROWS], value)
            tiles += [value[:, :128], value[:, 128:]]
        for i in range(0, STEP, 4):
            pairs = []
            for a in range(2):
                tile = tiles[i * 3 // 4 + a]
                lower = pltpu.roll(tile, LAYERS, 0)
                pairs.append(jnp.where(half, tile, swap(lower)))
                pairs.append(jnp.where(half, swap(tile), lower))
            tile = tiles[i * 3 // 4 + 2]
            shifts = [tile] + [pltpu.roll(tile, 128 - 32 * d, 1) for d in range(1, 4)]
            for j in range(4):
                turned = by_layer([shifts[(j - b) & 3] for b in range(LAYERS)])
                turned = jnp.where(quad == layer, turned, 0.0)
                re = turned[:LAYERS].sum(axis=0, keepdims=True)
                im = turned[LAYERS:].sum(axis=0, keepdims=True)
                out = jnp.where(sub < LAYERS, pairs[j], jnp.where(sub == LAYERS, re, im))
                sback[spot_rows(g * STEP + i + j, ROWS)] = out
        for i in range(STEP):
            if i > 0:
                incoming(g, i).start()
            else:

                @pl.when(g > 0)
                def _():
                    incoming(g, 0).start()

        return carry

    lax.fori_loop(0, PLANES // STEP, pick, 0)
    ret[spot_rows(me, ROWS)] = sback[0:ROWS]

    settle(ret.at[pl.ds(0, (PLANES - 1) * WIRE)], rt_recv.at[0])
    fetches[8].wait()
    lead = jnp.concatenate([ret[pl.ds(z, PLANES, stride=ROWS), :] for z in range(LAYERS)], 0)
    lead = lead * phase_a[:NG] + swap(lead) * (phase_a[NG:] * sign)
    rest_re = ret[pl.ds(LAYERS, PLANES, stride=ROWS), :]
    rest_im = ret[pl.ds(LAYERS + 1, PLANES, stride=ROWS), :]
    rest = []
    for value in (
        rest_re * phase_b[0] + rest_im * phase_b[1],
        rest_im * phase_b[0] - rest_re * phase_b[1],
    ):
        rest += [jnp.where(quad1 == b, value, 0.0) for b in range(LAYERS)]
    lead = dot3((lines_t[0, :, :NG], lines_t[1, :, :NG]), split(lead))
    lead = lead[:DEPTH] - swap(lead[DEPTH:]) * sign
    rest = dot3((lines_t[0], lines_t[1]), split(jnp.concatenate(rest, 0)))
    rest = rest + swap(rest)
    rest = rest + pltpu.roll(rest, 32, 1)
    picked = jnp.concatenate(
        [
            jnp.where(half1, lead, rest[:DEPTH]),
            jnp.where(half1, swap(lead), rest[DEPTH:]),
        ],
        0,
    )
    picked = pack(picked, pack_from) + terms[...]
    picked = jnp.where(jnp.concatenate([live, live], 0), picked, 0.0)
    for part in range(2):
        rows = picked[part * DEPTH : (part + 1) * DEPTH].T
        back[part] = rows.reshape(GROUPS, SLOT, DEPTH)

    copies = []
    for step in (2, 1, 3):
        other = (tg + step) & (GROUPS - 1)
        copy = pltpu.make_async_remote_copy(
            src_ref=back.at[:, other],
            dst_ref=result.at[:, tg],
            send_sem=out_send.at[step],
            recv_sem=out_recv.at[step],
            device_id=(other, me),
            device_id_type=MESH,
        )
        copy.start()
        copies.append(copy)
    own = pltpu.make_async_copy(back.at[:, tg], result.at[:, tg], stick_sem.at[0])
    own.start()
    settle(idents.at[pl.ds(1, PLANES - 1)], id_send.at[0])
    settle(send.at[pl.ds(0, (PLANES - 1) * WIRE)], pl_send.at[0])
    settle(sback.at[pl.ds(0, (PLANES - 1) * WIRE)], rt_send.at[0])
    own.wait()
    for copy in copies:
        copy.wait()


def local(coeffs, potential, stick_x, stick_y, stick_count, stick_offset):
    consts = [jnp.asarray(t) for t in tables()]
    vmem = lambda *shape, dtype=F32: pltpu.VMEM(shape, dtype)
    dma = pltpu.SemaphoreType.DMA
    args = (coeffs, potential, stick_x, stick_y, stick_count, stick_offset, *consts)
    return pl.pallas_call(
        kernel,
        out_shape=jax.ShapeDtypeStruct((2, GROUPS, SLOT, DEPTH), F32),
        in_specs=[pl.BlockSpec(memory_space=pltpu.HBM)] * len(args),
        out_specs=pl.BlockSpec(memory_space=pltpu.HBM),
        scratch_shapes=[
            vmem(2, GROUPS, SLOT, DEPTH),
            vmem(2, GROUPS, SLOT, DEPTH),
            vmem(4, SLOT, dtype=jnp.int32),
            vmem(8, 128),
            vmem(GROUPS, 8, 128),
            vmem(LAYERS, NG, NG),
        ]
        + [vmem(*t.shape, dtype=BF) for t in consts]
        + [
            vmem(PLANES * ROWS, 128),
            vmem(PLANES * ROWS, 128),
            vmem(2 * NG, 128),
            vmem(2, PLANES, 128),
            vmem(1, 1, 128),
            vmem(PLANES, 1, 128),
            vmem(PLANES // STEP, 2 * KEPT, STEP * 96, dtype=BF),
            vmem(2, KEPT // 2 * ROWS, KEPT),
            vmem(2, KEPT // 2 * ROWS, KEPT),
            vmem(KEPT // 2 * ROWS, 4 * KEPT, dtype=BF),
            vmem(2 * NG, LAYERS * KEPT),
            vmem(PLANES * ROWS, 128),
            vmem(PLANES * ROWS, 128),
            vmem(2, GROUPS, SLOT, DEPTH),
            vmem(PLANES * 3 // 4, ROWS, 128),
            vmem(2 * DEPTH, 128),
            dma((4,)),
            dma((10,)),
            dma((1,)),
            dma((1,)),
        ]
        + [dma((GROUPS,))] * 6
        + [dma((1,)), dma((PLANES // STEP,)), dma((1,)), dma((1,))],
        compiler_params=pltpu.CompilerParams(
            collective_id=0, has_side_effects=True, vmem_limit_bytes=62 * 1024 * 1024
        ),
    )(*args)


def solution(mesh):
    in_specs = (
        P(None, None, ("tg", "pl"), None),
        P("pl", None, None),
        P(("tg", "pl")),
        P(("tg", "pl")),
        P(("tg", "pl")),
        P(("tg", "pl")),
    )
    out_specs = P(None, None, ("tg", "pl"), None)
    return jax.shard_map(local, mesh=mesh, in_specs=in_specs, out_specs=out_specs, check_vma=False)
```

```python
import functools
import math

import jax
import jax.numpy as jnp
import numpy as np
from jax import lax
from jax.experimental import pallas as pl
from jax.experimental.pallas import tpu as pltpu
from jax.sharding import PartitionSpec as P

BF = jnp.bfloat16
F32 = jnp.float32
MESH = pl.DeviceIdType.MESH

NG = 256
DEPTH = 128
SLOT = 32
GROUPS = 4
PLANES = 64
LAYERS = 4
ROWS = 2 * LAYERS
KEPT = 128
MAIN = 20
WIRE = 6
STEP = 8


def halves(table):
    import ml_dtypes

    high = table.astype(ml_dtypes.bfloat16)
    low = (table - high.astype(np.float64)).astype(ml_dtypes.bfloat16)
    return np.stack([high, low])


def angles(rows, cols):
    return (np.multiply.outer(rows, cols) % NG) * (2.0 * math.pi / NG)


@functools.lru_cache(None)
def tables():
    planes = np.add.outer(np.arange(LAYERS), LAYERS * np.arange(PLANES)).reshape(-1)
    angle = angles(planes, np.arange(DEPTH))
    cos, sin = np.cos(angle), np.sin(angle)
    lines = np.block([[cos, -sin], [sin, cos]])
    angle = angles(planes, np.arange(NG))
    phase = np.concatenate([np.cos(angle), np.sin(angle)])
    freq = np.arange(KEPT) - KEPT // 2
    split = np.concatenate([freq[0::2], freq[1::2]])
    angle = angles(np.arange(NG), split)
    cos, sin = np.cos(angle), np.sin(angle)
    along_x = np.block([[cos, -sin], [sin, cos]])
    angle = angles(freq, np.arange(NG))
    cos, sin = np.cos(angle), np.sin(angle)
    along_y = np.block([[cos, sin], [-sin, cos]])
    scale = 1.0 / float(NG) ** 3
    return tuple(
        halves(t)
        for t in (lines, lines.T * scale, phase, along_x, along_x.T, along_y, along_y.T)
    )


def split(values):
    high = values.astype(BF)
    return high, (values - high.astype(F32)).astype(BF)


def dot(a, b):
    return jnp.dot(a, b, preferred_element_type=F32)


def pack(values, chosen):
    high, low = split(values)
    return dot(high, chosen) + dot(low, chosen)


def dot3(a, b):
    return dot(
        jnp.concatenate([a[0], a[0], a[1]], 1), jnp.concatenate([b[0], b[1], b[0]], 0)
    )


def settle(ref, semaphore):
    pltpu.make_async_copy(ref, ref, semaphore).wait()


def signed(index):
    return jnp.where(index < NG // 2, index, index - NG)


def quarter(index):
    index = index & 3
    one, zero = jnp.float32(1.0), jnp.float32(0.0)
    cos = jnp.where(index == 0, one, jnp.where(index == 2, -one, zero))
    sin = jnp.where(index == 1, one, jnp.where(index == 3, -one, zero))
    return cos, sin


def kernel(
    coeffs,
    potential,
    stick_x,
    stick_y,
    stick_count,
    stick_offset,
    lines_hbm,
    lines_t_hbm,
    phase_hbm,
    ax_hbm,
    axt_hbm,
    ay_hbm,
    ayt_hbm,
    result,
    group,
    coef,
    sticks,
    meta,
    metas,
    pot,
    lines,
    lines_t,
    phase,
    ax,
    axt,
    ay,
    ayt,
    send,
    recv,
    phase_a,
    phase_b,
    onehot,
    spread,
    plane,
    psi,
    fields,
    sback,
    ret,
    back,
    uppers,
    terms,
    stick_sem,
    local_sem,
    tg_send,
    tg_recv,
    out_send,
    out_recv,
    meta_send,
    meta_recv,
    pl_send,
    pl_recv,
    rt_send,
    rt_recv,
):
    tg = lax.axis_index("tg")
    me = lax.axis_index("pl")
    fetches = [
        pltpu.make_async_copy(src, dst, local_sem.at[i])
        for i, (src, dst) in enumerate(
            [
                (coeffs.at[:, tg], group.at[:, tg]),
                (phase_hbm, phase),
                (lines_hbm, lines),
                (ax_hbm, ax),
                (ay_hbm, ay),
                (potential, pot),
                (ayt_hbm, ayt),
                (axt_hbm, axt),
                (lines_t_hbm, lines_t),
                (coeffs, coef),
            ]
        )
    ]
    rows = [
        pltpu.make_async_copy(src, sticks.at[i], stick_sem.at[i])
        for i, src in enumerate((stick_x, stick_y, stick_count, stick_offset))
    ]
    for fetch in rows + fetches[9:]:
        fetch.start()

    barrier = pltpu.get_barrier_semaphore()
    for step in range(1, GROUPS):
        pl.semaphore_signal(
            barrier, inc=1, device_id=((tg + step) & (GROUPS - 1), me), device_id_type=MESH
        )

    def greet(step, carry):
        pl.semaphore_signal(
            barrier, inc=1, device_id=(tg, (me + step) & (PLANES - 1)), device_id_type=MESH
        )
        return carry

    lax.fori_loop(1, PLANES, greet, 0, unroll=True)
    for fetch in fetches[:9]:
        fetch.start()
    for row in rows:
        row.wait()
    mine = sticks[...]
    mine = jnp.concatenate([mine] * GROUPS, 1)
    index_x, index_y, counts, offsets = mine[0:1], mine[1:2], mine[2:3], mine[3:4]
    freq_x, freq_y = signed(index_x), signed(index_y)
    cell_x, cell_y = freq_x + KEPT // 2, freq_y + KEPT // 2
    cells = (cell_x >> 1) * 256 + (cell_x & 1) * 128 + cell_y
    cells = jnp.where(freq_x == KEPT // 2, 0, jnp.where(freq_y == KEPT // 2, 1, cells))
    cells = jnp.where(counts > 0, cells + 1, 0)
    offsets = jnp.where(counts > 0, offsets, 0)
    row_id = lax.broadcasted_iota(jnp.int32, (ROWS, 128), 0)
    mine = jnp.where(row_id == 3, freq_x * freq_x + freq_y * freq_y, 0)
    mine = jnp.where(row_id == 2, offsets, jnp.where(row_id == 1, counts, mine))
    mine = jnp.where(row_id == 0, cells, mine).astype(F32)
    owner = lax.broadcasted_iota(jnp.int32, (ROWS, 128), 1) // SLOT
    meta[...] = mine
    pl.semaphore_wait(barrier, GROUPS - 1 + PLANES - 1)

    fetches[9].wait()

    def packing(slot, place):
        spot = slot & (SLOT - 1)
        own = jnp.where(spot < MAIN, (slot // SLOT) * MAIN + spot, spot + (GROUPS - 1) * MAIN)
        return jnp.where(own == place, 1.0, 0.0).astype(BF)

    along = lax.broadcasted_iota(jnp.int32, (128, 128), 0)
    across = lax.broadcasted_iota(jnp.int32, (128, 128), 1)
    pack_to = jnp.concatenate(
        [packing(along, across & 63), packing(along, 64 + (across & 31))], 1
    )
    pack_from = packing(across, along)
    lane = lax.broadcasted_iota(jnp.int32, (ROWS, 128), 1)
    sub = lax.broadcasted_iota(jnp.int32, (ROWS, 128), 0)
    half = lane < 64
    half1, quad1 = half[0:1], lane[0:1] // 32
    quad = lane // 32
    sign = jnp.where(half1, 1.0, -1.0)
    swap = lambda v: pltpu.roll(v, 64, 1)

    layer = sub & (LAYERS - 1)

    def by_layer(values):
        low = jnp.where(layer == 0, values[0], values[1])
        return jnp.where(layer < 2, low, jnp.where(layer == 2, values[2], values[3]))

    def diagonal(rows):
        out = rows[0:PLANES]
        for b in range(1, LAYERS):
            out = jnp.where(quad1 == b, rows[b * PLANES : (b + 1) * PLANES], out)
        return out

    copies = []
    for step in (2, 1, 3):
        other = (tg + step) & (GROUPS - 1)
        for src, dst, sems in (
            (meta, metas.at[step], (meta_send, meta_recv)),
            (coef.at[:, other], group.at[:, tg], (tg_send, tg_recv)),
        ):
            copy = pltpu.make_async_remote_copy(
                src_ref=src,
                dst_ref=dst,
                send_sem=sems[0].at[step],
                recv_sem=sems[1].at[step],
                device_id=(other, me),
                device_id_type=MESH,
            )
            copy.start()
            copies.append(copy)
    for copy in copies[0::2]:
        copy.wait()
    info = mine
    for step in range(1, GROUPS):
        info = jnp.where(owner == (tg - step) & (GROUPS - 1), metas[step], info)
    count = info[1:2]
    packed = pack(info, pack_to)
    ids, offset = packed[0:1] - 1.0, packed[2:3]
    names = jnp.where(half1, ids[:, 0:128], ids[:, 128:256])

    def peer(ring, spot, sign):
        along_z = ((ring + 1) >> 1) * (2 * (ring & 1) - 1)
        x = ((me >> 4) + sign * (spot >> 1)) & 3
        z = ((me >> 1) + sign * along_z) & 7
        return x * 16 + z * 2 + ((me + spot) & 1)

    fetches[1].wait()
    steps = lax.broadcasted_iota(jnp.int32, (NG, 128), 0).astype(F32)
    chosen = jnp.concatenate(
        [jnp.where(steps == offset[:, t * 128 : (t + 1) * 128], 1.0, 0.0) for t in range(2)], 1
    ).astype(BF)
    turns = dot(phase[0], chosen) + dot(phase[1], chosen)
    phase_a[...] = turns[:, :128]
    for trig in range(2):
        phase_b[trig] = diagonal(turns[trig * NG : (trig + 1) * NG, 128:])
    fetches[0].wait()
    fetches[2].wait()
    for copy in copies[1::2]:
        copy.wait()

    live = steps[:DEPTH] < count
    parts = []
    for part in range(2):
        rows = group[part].reshape(GROUPS * SLOT, DEPTH)
        parts.append(jnp.where(live, rows.T, 0.0))
    masked = jnp.concatenate(parts, 0)
    sides = []
    for value in split(masked):
        value = dot(value, pack_to)
        re, im = value[:DEPTH, :128], value[DEPTH:, :128]
        left = jnp.concatenate([jnp.where(half1, re, im), jnp.where(half1, im, -re)], 0)
        sides.append(jnp.concatenate([left, value[:, 128:]], 1).astype(BF))
    both = dot3((lines[0], lines[1]), sides)
    moved = both[:NG, :128] * phase_a[:NG] - both[NG:, :128] * phase_a[NG:]
    for z in range(LAYERS):
        send[pl.ds(z, PLANES, stride=ROWS), :] = moved[z * PLANES : (z + 1) * PLANES]
    re, im = diagonal(both[:NG, 128:]), diagonal(both[NG:, 128:])
    send[pl.ds(LAYERS, PLANES, stride=ROWS), :] = re * phase_b[0] - im * phase_b[1]
    send[pl.ds(LAYERS + 1, PLANES, stride=ROWS), :] = im * phase_b[0] + re * phase_b[1]
    send[pl.ds(WIRE, PLANES, stride=ROWS), :] = jnp.broadcast_to(names, (PLANES, 128))

    def spot_rows(index, rows):
        return pl.ds(pl.multiple_of(index * ROWS, ROWS), rows)

    def outgoing(ring, spot):
        other = peer(ring, spot, 1)
        return pltpu.make_async_remote_copy(
            src_ref=send.at[spot_rows(other, WIRE + 1)],
            dst_ref=recv.at[spot_rows(ring * STEP + spot, WIRE + 1)],
            send_sem=pl_send.at[0],
            recv_sem=pl_recv.at[ring],
            device_id=(tg, other),
            device_id_type=MESH,
        )

    for ring in range(PLANES // STEP):
        for spot in range(0 if ring else 1, STEP):
            outgoing(ring, spot).start()
    recv[0:ROWS] = send[spot_rows(me, ROWS)]

    column = lax.broadcasted_iota(jnp.int32, (2 * KEPT, 128), 0).astype(F32).astype(BF)
    second = jnp.where(lax.broadcasted_iota(jnp.int32, (16, 128), 0) >= 8, 1.0, 0.0).astype(F32)
    one, zero = jnp.ones((), BF), jnp.zeros((), BF)

    def place(g, carry):
        @pl.when(g == 0)
        def _():
            settle(recv.at[pl.ds(0, (STEP - 1) * (WIRE + 1))], pl_recv.at[0])

        @pl.when(g > 0)
        def _():
            settle(recv.at[pl.ds(0, STEP * (WIRE + 1))], pl_recv.at[g])

        block = recv[spot_rows(g * STEP, STEP * ROWS)]
        left, right = [], []
        tiles = []
        for i in range(0, STEP, 4):
            rows = [block[(i + j) * ROWS : (i + j + 1) * ROWS] for j in range(4)]
            ids8 = [jnp.broadcast_to(rows[j][WIRE : WIRE + 1], (ROWS, 128)) for j in range(4)]
            for a in (0, 2):
                top = jnp.where(half, rows[a], swap(rows[a + 1]))
                low = jnp.where(half, swap(rows[a]), rows[a + 1])
                tile = jnp.where(sub < LAYERS, top, pltpu.roll(low, LAYERS, 0))
                tiles.append((tile, jnp.where(half, ids8[a], swap(ids8[a + 1]))))
            wide = [
                jnp.where(sub < LAYERS, row[LAYERS : LAYERS + 1], row[LAYERS + 1 : LAYERS + 2])
                for row in rows
            ]
            name = jnp.zeros((ROWS, 128), F32)
            for j in range(4):
                near = ids8[j] if j == 2 else pltpu.roll(ids8[j], (32 * j - 64) % 128, 1)
                name = jnp.where(quad == j, near, name)
            tile = by_layer(wide)
            for d in range(1, 4):
                shifted = pltpu.roll(by_layer(wide[d:] + wide[:d]), 32 * d, 1)
                tile = jnp.where(quad == (layer + d) & 3, shifted, tile)
            tiles.append((tile, name))
        for i, (tile, name) in enumerate(tiles):
            high, low = split(tile)
            upper = jnp.floor(name * (1.0 / 256.0))
            lower = (name - 256.0 * upper)[0:1].astype(BF)
            uppers[g * len(tiles) + i] = upper
            upper = jnp.concatenate([upper, upper], 0)
            match = (upper - second).astype(BF)
            pieces = []
            for value in (high, low):
                value = jnp.concatenate([value, value], 0)
                for j in range(KEPT // 4):
                    pieces.append(jnp.where(match == jnp.asarray(2.0 * j, BF), value, zero))
            left.append(jnp.concatenate(pieces, 0))
            right.append(jnp.where(column == lower, one, zero))
        left = jnp.concatenate(left, 1)
        right = jnp.concatenate(right, 1)
        onehot[g] = right
        total = lax.dot_general(
            left, right, (((1,), (1,)), ((), ())), preferred_element_type=F32
        )
        total = total[: KEPT // 2 * ROWS] + total[KEPT // 2 * ROWS :]

        @pl.when(g == 0)
        def _():
            spread[0] = total[:, :KEPT]
            spread[1] = total[:, KEPT:]

        @pl.when(g > 0)
        def _():
            spread[0] += total[:, :KEPT]
            spread[1] += total[:, KEPT:]

        return carry

    lax.fori_loop(0, PLANES // STEP, place, 0)

    corner = spread[0, 0:ROWS]
    edge_x = jnp.where(lane == 0, corner, 0.0).sum(axis=1, keepdims=True)
    edge_y = jnp.where(lane == 1, corner, 0.0).sum(axis=1, keepdims=True)
    spread[0, 0:ROWS] = jnp.where(lane < 2, 0.0, corner)
    fetches[3].wait()
    columns = []
    for z in range(LAYERS):
        stack = []
        for part in range(2):
            for parity in range(2):
                stack.append(spread[parity, pl.ds(part * LAYERS + z, KEPT // 2, stride=ROWS), :])
        columns.append(jnp.concatenate(stack, 0))
    mixed = dot3((ax[0], ax[1]), split(jnp.concatenate(columns, 1)))
    fields[...] = mixed

    fetches[4].wait()
    fetches[5].wait()
    fetches[6].wait()
    cos_x, sin_x = quarter(lax.broadcasted_iota(jnp.int32, (NG, KEPT), 0))
    cos_y, sin_y = quarter(lax.broadcasted_iota(jnp.int32, (1, NG), 1))
    got_x = jnp.zeros((ROWS, 128), F32)
    got_y = jnp.zeros((ROWS, 128), F32)
    centre = lax.broadcasted_iota(jnp.int32, (1, KEPT), 1) == KEPT // 2
    for z in range(LAYERS):
        re = fields[0:NG, z * KEPT : (z + 1) * KEPT]
        im = fields[NG : 2 * NG, z * KEPT : (z + 1) * KEPT]
        er = jnp.where(centre, edge_x[z : z + 1], 0.0)
        ei = jnp.where(centre, edge_x[LAYERS + z : LAYERS + z + 1], 0.0)
        re = re + (cos_x * er - sin_x * ei)
        im = im + (sin_x * er + cos_x * ei)
        wave = dot3(split(jnp.concatenate([re, im], 1)), (ay[0], ay[1]))
        er = edge_y[z : z + 1]
        ei = edge_y[LAYERS + z : LAYERS + z + 1]
        local = pot[z]
        re = (wave[:, :NG] + (cos_y * er - sin_y * ei)) * local
        im = (wave[:, NG:] + (sin_y * er + cos_y * ei)) * local
        sum_re = re.sum(axis=0, keepdims=True)
        sum_im = im.sum(axis=0, keepdims=True)
        er = (cos_y * sum_re + sin_y * sum_im).sum(axis=1, keepdims=True)
        ei = (cos_y * sum_im - sin_y * sum_re).sum(axis=1, keepdims=True)
        got_y = jnp.where(row_id == z, er, jnp.where(row_id == LAYERS + z, ei, got_y))
        mid = dot3(split(jnp.concatenate([re, im], 1)), (ayt[0], ayt[1]))
        re, im = mid[:, :KEPT], mid[:, KEPT:]
        er = (cos_x * re + sin_x * im).sum(axis=0, keepdims=True)
        ei = (cos_x * im - sin_x * re).sum(axis=0, keepdims=True)
        er = jnp.where(centre, er, 0.0).sum(axis=1, keepdims=True)
        ei = jnp.where(centre, ei, 0.0).sum(axis=1, keepdims=True)
        got_x = jnp.where(row_id == z, er, jnp.where(row_id == LAYERS + z, ei, got_x))
        fields[0:NG, z * KEPT : (z + 1) * KEPT] = re
        fields[NG : 2 * NG, z * KEPT : (z + 1) * KEPT] = im
    fetches[7].wait()
    mixed = dot3((axt[0], axt[1]), split(fields[...]))
    for z in range(LAYERS):
        for part in range(2):
            block = mixed[part * KEPT : (part + 1) * KEPT, z * KEPT : (z + 1) * KEPT]
            for parity in range(2):
                plane[parity, pl.ds(part * LAYERS + z, KEPT // 2, stride=ROWS), :] = block[
                    parity * (KEPT // 2) : (parity + 1) * (KEPT // 2)
                ]
    corner = plane[0, 0:ROWS]
    plane[0, 0:ROWS] = jnp.where(lane == 0, got_x, jnp.where(lane == 1, got_y, corner))
    for parity in range(2):
        high, low = split(plane[parity])
        psi[:, parity * KEPT : (parity + 1) * KEPT] = high
        psi[:, (2 + parity) * KEPT : (3 + parity) * KEPT] = low

    def incoming(ring, spot):
        other = peer(ring, spot, -1)
        return pltpu.make_async_remote_copy(
            src_ref=sback.at[spot_rows(ring * STEP + spot, WIRE)],
            dst_ref=ret.at[spot_rows(me, WIRE)],
            send_sem=rt_send.at[0],
            recv_sem=rt_recv.at[0],
            device_id=(tg, other),
            device_id_type=MESH,
        )

    def pick(turn, carry):
        g = PLANES // STEP - 1 - turn
        tiles = []
        for i in range(0, STEP * 3 // 4, 2):
            right = onehot[g, :, i * 128 : (i + 2) * 128]
            found = dot(psi[...], jnp.concatenate([right, right], 0))
            upper = jnp.concatenate(
                [uppers[g * (STEP * 3 // 4) + i + e] for e in range(2)], 1
            )
            value = jnp.zeros((ROWS, 256), F32)
            for j in range(KEPT // 2):
                value = jnp.where(upper == float(j), found[j * ROWS : (j + 1) * ROWS], value)
            tiles += [value[:, :128], value[:, 128:]]
        for i in range(0, STEP, 4):
            pairs = []
            for a in range(2):
                tile = tiles[i * 3 // 4 + a]
                lower = pltpu.roll(tile, LAYERS, 0)
                pairs.append(jnp.where(half, tile, swap(lower)))
                pairs.append(jnp.where(half, swap(tile), lower))
            tile = tiles[i * 3 // 4 + 2]
            shifts = [tile] + [pltpu.roll(tile, 128 - 32 * d, 1) for d in range(1, 4)]
            for j in range(4):
                turned = by_layer([shifts[(j - b) & 3] for b in range(LAYERS)])
                turned = jnp.where(quad == layer, turned, 0.0)
                re = turned[:LAYERS].sum(axis=0, keepdims=True)
                im = turned[LAYERS:].sum(axis=0, keepdims=True)
                out = jnp.where(sub < LAYERS, pairs[j], jnp.where(sub == LAYERS, re, im))
                sback[spot_rows(g * STEP + i + j, ROWS)] = out
        for i in range(STEP):
            if i > 0:
                incoming(g, i).start()
            else:

                @pl.when(g > 0)
                def _():
                    incoming(g, 0).start()

        return carry

    lax.fori_loop(0, PLANES // STEP, pick, 0)
    ret[spot_rows(me, ROWS)] = sback[0:ROWS]

    height = steps[:DEPTH] + info[2:3]
    height = jnp.where(height >= float(NG), height - float(NG), height)
    height = jnp.where(height >= float(NG // 2), height - float(NG), height)
    kinetic = (0.5 * (32.0 / (NG * NG))) * (info[3:4] + height * height)
    terms[...] = jnp.concatenate([kinetic, kinetic], 0) * masked

    settle(ret.at[pl.ds(0, (PLANES - 1) * WIRE)], rt_recv.at[0])
    fetches[8].wait()
    lead = jnp.concatenate([ret[pl.ds(z, PLANES, stride=ROWS), :] for z in range(LAYERS)], 0)
    lead = lead * phase_a[:NG] + swap(lead) * (phase_a[NG:] * sign)
    rest_re = ret[pl.ds(LAYERS, PLANES, stride=ROWS), :]
    rest_im = ret[pl.ds(LAYERS + 1, PLANES, stride=ROWS), :]
    rest = []
    for value in (
        rest_re * phase_b[0] + rest_im * phase_b[1],
        rest_im * phase_b[0] - rest_re * phase_b[1],
    ):
        rest += [jnp.where(quad1 == b, value, 0.0) for b in range(LAYERS)]
    lead = dot3((lines_t[0, :, :NG], lines_t[1, :, :NG]), split(lead))
    lead = lead[:DEPTH] - swap(lead[DEPTH:]) * sign
    rest = dot3((lines_t[0], lines_t[1]), split(jnp.concatenate(rest, 0)))
    rest = rest + swap(rest)
    rest = rest + pltpu.roll(rest, 32, 1)
    picked = jnp.concatenate(
        [
            jnp.where(half1, lead, rest[:DEPTH]),
            jnp.where(half1, swap(lead), rest[DEPTH:]),
        ],
        0,
    )
    picked = pack(picked, pack_from) + terms[...]
    picked = jnp.where(jnp.concatenate([live, live], 0), picked, 0.0)
    for part in range(2):
        rows = picked[part * DEPTH : (part + 1) * DEPTH].T
        back[part] = rows.reshape(GROUPS, SLOT, DEPTH)

    copies = []
    for step in (2, 1, 3):
        other = (tg + step) & (GROUPS - 1)
        copy = pltpu.make_async_remote_copy(
            src_ref=back.at[:, other],
            dst_ref=result.at[:, tg],
            send_sem=out_send.at[step],
            recv_sem=out_recv.at[step],
            device_id=(other, me),
            device_id_type=MESH,
        )
        copy.start()
        copies.append(copy)
    own = pltpu.make_async_copy(back.at[:, tg], result.at[:, tg], stick_sem.at[0])
    own.start()
    settle(send.at[pl.ds(0, (PLANES - 1) * (WIRE + 1))], pl_send.at[0])
    settle(sback.at[pl.ds(0, (PLANES - 1) * WIRE)], rt_send.at[0])
    own.wait()
    for copy in copies:
        copy.wait()


def local(coeffs, potential, stick_x, stick_y, stick_count, stick_offset):
    consts = [jnp.asarray(t) for t in tables()]
    vmem = lambda *shape, dtype=F32: pltpu.VMEM(shape, dtype)
    dma = pltpu.SemaphoreType.DMA
    args = (coeffs, potential, stick_x, stick_y, stick_count, stick_offset, *consts)
    return pl.pallas_call(
        kernel,
        out_shape=jax.ShapeDtypeStruct((2, GROUPS, SLOT, DEPTH), F32),
        in_specs=[pl.BlockSpec(memory_space=pltpu.HBM)] * len(args),
        out_specs=pl.BlockSpec(memory_space=pltpu.HBM),
        scratch_shapes=[
            vmem(2, GROUPS, SLOT, DEPTH),
            vmem(2, GROUPS, SLOT, DEPTH),
            vmem(4, SLOT, dtype=jnp.int32),
            vmem(8, 128),
            vmem(GROUPS, 8, 128),
            vmem(LAYERS, NG, NG),
        ]
        + [vmem(*t.shape, dtype=BF) for t in consts]
        + [
            vmem(PLANES * ROWS, 128),
            vmem(PLANES * ROWS, 128),
            vmem(2 * NG, 128),
            vmem(2, PLANES, 128),
            vmem(PLANES // STEP, 2 * KEPT, STEP * 96, dtype=BF),
            vmem(2, KEPT // 2 * ROWS, KEPT),
            vmem(2, KEPT // 2 * ROWS, KEPT),
            vmem(KEPT // 2 * ROWS, 4 * KEPT, dtype=BF),
            vmem(2 * NG, LAYERS * KEPT),
            vmem(PLANES * ROWS, 128),
            vmem(PLANES * ROWS, 128),
            vmem(2, GROUPS, SLOT, DEPTH),
            vmem(PLANES * 3 // 4, ROWS, 128),
            vmem(2 * DEPTH, 128),
            dma((4,)),
            dma((10,)),
        ]
        + [dma((GROUPS,))] * 6
        + [dma((1,)), dma((PLANES // STEP,)), dma((1,)), dma((1,))],
        compiler_params=pltpu.CompilerParams(
            collective_id=0, has_side_effects=True, vmem_limit_bytes=62 * 1024 * 1024
        ),
    )(*args)


def solution(mesh):
    in_specs = (
        P(None, None, ("tg", "pl"), None),
        P("pl", None, None),
        P(("tg", "pl")),
        P(("tg", "pl")),
        P(("tg", "pl")),
        P(("tg", "pl")),
    )
    out_specs = P(None, None, ("tg", "pl"), None)
    return jax.shard_map(local, mesh=mesh, in_specs=in_specs, out_specs=out_specs, check_vma=False)
```

```python
import functools
import math

import jax
import jax.numpy as jnp
import numpy as np
from jax import lax
from jax.experimental import pallas as pl
from jax.experimental.pallas import tpu as pltpu
from jax.sharding import PartitionSpec as P

BF = jnp.bfloat16
F32 = jnp.float32
MESH = pl.DeviceIdType.MESH

NG = 256
DEPTH = 128
SLOT = 32
GROUPS = 4
PLANES = 64
LAYERS = 4
ROWS = 2 * LAYERS
KEPT = 128
MAIN = 20
WIRE = 6
STEP = 8


def halves(table):
    import ml_dtypes

    high = table.astype(ml_dtypes.bfloat16)
    low = (table - high.astype(np.float64)).astype(ml_dtypes.bfloat16)
    return np.stack([high, low])


def angles(rows, cols):
    return (np.multiply.outer(rows, cols) % NG) * (2.0 * math.pi / NG)


@functools.lru_cache(None)
def tables():
    planes = np.add.outer(np.arange(LAYERS), LAYERS * np.arange(PLANES)).reshape(-1)
    angle = angles(planes, np.arange(DEPTH))
    cos, sin = np.cos(angle), np.sin(angle)
    lines = np.block([[cos, -sin], [sin, cos]])
    angle = angles(planes, np.arange(NG))
    phase = np.concatenate([np.cos(angle), np.sin(angle)])
    freq = np.arange(KEPT) - KEPT // 2
    split = np.concatenate([freq[0::2], freq[1::2]])
    angle = angles(np.arange(NG), split)
    cos, sin = np.cos(angle), np.sin(angle)
    along_x = np.block([[cos, -sin], [sin, cos]])
    angle = angles(freq, np.arange(NG))
    cos, sin = np.cos(angle), np.sin(angle)
    along_y = np.block([[cos, sin], [-sin, cos]])
    scale = 1.0 / float(NG) ** 3
    return tuple(
        halves(t)
        for t in (lines, lines.T * scale, phase, along_x, along_x.T, along_y, along_y.T)
    )


def split(values):
    high = values.astype(BF)
    return high, (values - high.astype(F32)).astype(BF)


def dot(a, b):
    return jnp.dot(a, b, preferred_element_type=F32)


def pack(values, chosen):
    high, low = split(values)
    return dot(high, chosen) + dot(low, chosen)


def dot3(a, b):
    return dot(
        jnp.concatenate([a[0], a[0], a[1]], 1), jnp.concatenate([b[0], b[1], b[0]], 0)
    )


def settle(ref, semaphore):
    pltpu.make_async_copy(ref, ref, semaphore).wait()


def signed(index):
    return jnp.where(index < NG // 2, index, index - NG)


def quarter(index):
    index = index & 3
    one, zero = jnp.float32(1.0), jnp.float32(0.0)
    cos = jnp.where(index == 0, one, jnp.where(index == 2, -one, zero))
    sin = jnp.where(index == 1, one, jnp.where(index == 3, -one, zero))
    return cos, sin


def kernel(
    coeffs,
    potential,
    stick_x,
    stick_y,
    stick_count,
    stick_offset,
    lines_hbm,
    lines_t_hbm,
    phase_hbm,
    ax_hbm,
    axt_hbm,
    ay_hbm,
    ayt_hbm,
    result,
    group,
    coef,
    sticks,
    meta,
    metas,
    pot,
    lines,
    lines_t,
    phase,
    ax,
    axt,
    ay,
    ayt,
    send,
    recv,
    phase_a,
    phase_b,
    onehot,
    spread,
    plane,
    psi,
    fields,
    sback,
    ret,
    back,
    uppers,
    terms,
    stick_sem,
    local_sem,
    tg_send,
    tg_recv,
    out_send,
    out_recv,
    meta_send,
    meta_recv,
    pl_send,
    pl_recv,
    rt_send,
    rt_recv,
):
    tg = lax.axis_index("tg")
    me = lax.axis_index("pl")
    fetches = [
        pltpu.make_async_copy(src, dst, local_sem.at[i])
        for i, (src, dst) in enumerate(
            [
                (coeffs.at[:, tg], group.at[:, tg]),
                (phase_hbm, phase),
                (lines_hbm, lines),
                (ax_hbm, ax),
                (ay_hbm, ay),
                (potential, pot),
                (ayt_hbm, ayt),
                (axt_hbm, axt),
                (lines_t_hbm, lines_t),
                (coeffs, coef),
            ]
        )
    ]
    rows = [
        pltpu.make_async_copy(src, sticks.at[i], stick_sem.at[i])
        for i, src in enumerate((stick_x, stick_y, stick_count, stick_offset))
    ]
    for fetch in rows + fetches[9:]:
        fetch.start()

    barrier = pltpu.get_barrier_semaphore()
    for step in range(1, GROUPS):
        pl.semaphore_signal(
            barrier, inc=1, device_id=((tg + step) & (GROUPS - 1), me), device_id_type=MESH
        )

    def greet(step, carry):
        pl.semaphore_signal(
            barrier, inc=1, device_id=(tg, (me + step) & (PLANES - 1)), device_id_type=MESH
        )
        return carry

    lax.fori_loop(1, PLANES, greet, 0, unroll=True)
    for fetch in fetches[:9]:
        fetch.start()
    for row in rows:
        row.wait()
    mine = sticks[...]
    mine = jnp.concatenate([mine] * GROUPS, 1)
    index_x, index_y, counts, offsets = mine[0:1], mine[1:2], mine[2:3], mine[3:4]
    freq_x, freq_y = signed(index_x), signed(index_y)
    cell_x, cell_y = freq_x + KEPT // 2, freq_y + KEPT // 2
    cells = (cell_x >> 1) * 256 + (cell_x & 1) * 128 + cell_y
    cells = jnp.where(freq_x == KEPT // 2, 0, jnp.where(freq_y == KEPT // 2, 1, cells))
    cells = jnp.where(counts > 0, cells + 1, 0)
    offsets = jnp.where(counts > 0, offsets, 0)
    row_id = lax.broadcasted_iota(jnp.int32, (ROWS, 128), 0)
    mine = jnp.where(row_id == 3, freq_x * freq_x + freq_y * freq_y, 0)
    mine = jnp.where(row_id == 2, offsets, jnp.where(row_id == 1, counts, mine))
    mine = jnp.where(row_id == 0, cells, mine).astype(F32)
    owner = lax.broadcasted_iota(jnp.int32, (ROWS, 128), 1) // SLOT
    meta[...] = mine
    pl.semaphore_wait(barrier, GROUPS - 1 + PLANES - 1)

    fetches[9].wait()

    def packing(slot, place):
        spot = slot & (SLOT - 1)
        own = jnp.where(spot < MAIN, (slot // SLOT) * MAIN + spot, spot + (GROUPS - 1) * MAIN)
        return jnp.where(own == place, 1.0, 0.0).astype(BF)

    along = lax.broadcasted_iota(jnp.int32, (128, 128), 0)
    across = lax.broadcasted_iota(jnp.int32, (128, 128), 1)
    pack_to = jnp.concatenate(
        [packing(along, across & 63), packing(along, 64 + (across & 31))], 1
    )
    pack_from = packing(across, along)
    lane = lax.broadcasted_iota(jnp.int32, (ROWS, 128), 1)
    sub = lax.broadcasted_iota(jnp.int32, (ROWS, 128), 0)
    half = lane < 64
    half1, quad1 = half[0:1], lane[0:1] // 32
    quad = lane // 32
    sign = jnp.where(half1, 1.0, -1.0)
    swap = lambda v: pltpu.roll(v, 64, 1)

    layer = sub & (LAYERS - 1)

    def by_layer(values):
        low = jnp.where(layer == 0, values[0], values[1])
        return jnp.where(layer < 2, low, jnp.where(layer == 2, values[2], values[3]))

    def diagonal(rows):
        out = rows[0:PLANES]
        for b in range(1, LAYERS):
            out = jnp.where(quad1 == b, rows[b * PLANES : (b + 1) * PLANES], out)
        return out

    copies = []
    for step in (2, 1, 3):
        other = (tg + step) & (GROUPS - 1)
        for src, dst, sems in (
            (meta, metas.at[step], (meta_send, meta_recv)),
            (coef.at[:, other], group.at[:, tg], (tg_send, tg_recv)),
        ):
            copy = pltpu.make_async_remote_copy(
                src_ref=src,
                dst_ref=dst,
                send_sem=sems[0].at[step],
                recv_sem=sems[1].at[step],
                device_id=(other, me),
                device_id_type=MESH,
            )
            copy.start()
            copies.append(copy)
    for copy in copies[0::2]:
        copy.wait()
    info = mine
    for step in range(1, GROUPS):
        info = jnp.where(owner == (tg - step) & (GROUPS - 1), metas[step], info)
    count = info[1:2]
    packed = pack(info, pack_to)
    ids, offset = packed[0:1] - 1.0, packed[2:3]
    names = jnp.where(half1, ids[:, 0:128], ids[:, 128:256])

    def peer(ring, spot, sign):
        along_z = ((ring + 1) >> 1) * (2 * (ring & 1) - 1)
        x = ((me >> 4) + sign * (spot >> 1)) & 3
        z = ((me >> 1) + sign * along_z) & 7
        return x * 16 + z * 2 + ((me + spot) & 1)

    fetches[1].wait()
    steps = lax.broadcasted_iota(jnp.int32, (NG, 128), 0).astype(F32)
    chosen = jnp.concatenate(
        [jnp.where(steps == offset[:, t * 128 : (t + 1) * 128], 1.0, 0.0) for t in range(2)], 1
    ).astype(BF)
    turns = dot(phase[0], chosen) + dot(phase[1], chosen)
    phase_a[...] = turns[:, :128]
    for trig in range(2):
        phase_b[trig] = diagonal(turns[trig * NG : (trig + 1) * NG, 128:])
    fetches[0].wait()
    fetches[2].wait()
    for copy in copies[1::2]:
        copy.wait()

    live = steps[:DEPTH] < count
    parts = []
    for part in range(2):
        rows = group[part].reshape(GROUPS * SLOT, DEPTH)
        parts.append(jnp.where(live, rows.T, 0.0))
    masked = jnp.concatenate(parts, 0)
    sides = []
    for value in split(masked):
        value = dot(value, pack_to)
        re, im = value[:DEPTH, :128], value[DEPTH:, :128]
        left = jnp.concatenate([jnp.where(half1, re, im), jnp.where(half1, im, -re)], 0)
        sides.append(jnp.concatenate([left, value[:, 128:]], 1).astype(BF))
    both = dot3((lines[0], lines[1]), sides)
    moved = both[:NG, :128] * phase_a[:NG] - both[NG:, :128] * phase_a[NG:]
    for z in range(LAYERS):
        send[pl.ds(z, PLANES, stride=ROWS), :] = moved[z * PLANES : (z + 1) * PLANES]
    re, im = diagonal(both[:NG, 128:]), diagonal(both[NG:, 128:])
    send[pl.ds(LAYERS, PLANES, stride=ROWS), :] = re * phase_b[0] - im * phase_b[1]
    send[pl.ds(LAYERS + 1, PLANES, stride=ROWS), :] = im * phase_b[0] + re * phase_b[1]
    send[pl.ds(WIRE, PLANES, stride=ROWS), :] = jnp.broadcast_to(names, (PLANES, 128))

    def spot_rows(index, rows):
        return pl.ds(pl.multiple_of(index * ROWS, ROWS), rows)

    def outgoing(ring, spot):
        other = peer(ring, spot, 1)
        return pltpu.make_async_remote_copy(
            src_ref=send.at[spot_rows(other, WIRE + 1)],
            dst_ref=recv.at[spot_rows(ring * STEP + spot, WIRE + 1)],
            send_sem=pl_send.at[0],
            recv_sem=pl_recv.at[ring],
            device_id=(tg, other),
            device_id_type=MESH,
        )

    for ring in range(PLANES // STEP):
        for spot in (4, 5, 6, 7, 2, 3, 1, 0)[: STEP if ring else STEP - 1]:
            outgoing(ring, spot).start()
    recv[0:ROWS] = send[spot_rows(me, ROWS)]

    column = lax.broadcasted_iota(jnp.int32, (2 * KEPT, 128), 0).astype(F32).astype(BF)
    second = jnp.where(lax.broadcasted_iota(jnp.int32, (16, 128), 0) >= 8, 1.0, 0.0).astype(F32)
    one, zero = jnp.ones((), BF), jnp.zeros((), BF)

    def place(g, carry):
        @pl.when(g == 0)
        def _():
            settle(recv.at[pl.ds(0, (STEP - 1) * (WIRE + 1))], pl_recv.at[0])

        @pl.when(g > 0)
        def _():
            settle(recv.at[pl.ds(0, STEP * (WIRE + 1))], pl_recv.at[g])

        block = recv[spot_rows(g * STEP, STEP * ROWS)]
        left, right = [], []
        tiles = []
        for i in range(0, STEP, 4):
            rows = [block[(i + j) * ROWS : (i + j + 1) * ROWS] for j in range(4)]
            ids8 = [jnp.broadcast_to(rows[j][WIRE : WIRE + 1], (ROWS, 128)) for j in range(4)]
            for a in (0, 2):
                top = jnp.where(half, rows[a], swap(rows[a + 1]))
                low = jnp.where(half, swap(rows[a]), rows[a + 1])
                tile = jnp.where(sub < LAYERS, top, pltpu.roll(low, LAYERS, 0))
                tiles.append((tile, jnp.where(half, ids8[a], swap(ids8[a + 1]))))
            wide = [
                jnp.where(sub < LAYERS, row[LAYERS : LAYERS + 1], row[LAYERS + 1 : LAYERS + 2])
                for row in rows
            ]
            name = jnp.zeros((ROWS, 128), F32)
            for j in range(4):
                near = ids8[j] if j == 2 else pltpu.roll(ids8[j], (32 * j - 64) % 128, 1)
                name = jnp.where(quad == j, near, name)
            tile = by_layer(wide)
            for d in range(1, 4):
                shifted = pltpu.roll(by_layer(wide[d:] + wide[:d]), 32 * d, 1)
                tile = jnp.where(quad == (layer + d) & 3, shifted, tile)
            tiles.append((tile, name))
        for i, (tile, name) in enumerate(tiles):
            high, low = split(tile)
            upper = jnp.floor(name * (1.0 / 256.0))
            lower = (name - 256.0 * upper)[0:1].astype(BF)
            uppers[g * len(tiles) + i] = upper
            upper = jnp.concatenate([upper, upper], 0)
            match = (upper - second).astype(BF)
            pieces = []
            for value in (high, low):
                value = jnp.concatenate([value, value], 0)
                for j in range(KEPT // 4):
                    pieces.append(jnp.where(match == jnp.asarray(2.0 * j, BF), value, zero))
            left.append(jnp.concatenate(pieces, 0))
            right.append(jnp.where(column == lower, one, zero))
        left = jnp.concatenate(left, 1)
        right = jnp.concatenate(right, 1)
        onehot[g] = right
        total = lax.dot_general(
            left, right, (((1,), (1,)), ((), ())), preferred_element_type=F32
        )
        total = total[: KEPT // 2 * ROWS] + total[KEPT // 2 * ROWS :]

        @pl.when(g == 0)
        def _():
            spread[0] = total[:, :KEPT]
            spread[1] = total[:, KEPT:]

        @pl.when(g > 0)
        def _():
            spread[0] += total[:, :KEPT]
            spread[1] += total[:, KEPT:]

        return carry

    lax.fori_loop(0, PLANES // STEP, place, 0)

    corner = spread[0, 0:ROWS]
    edge_x = jnp.where(lane == 0, corner, 0.0).sum(axis=1, keepdims=True)
    edge_y = jnp.where(lane == 1, corner, 0.0).sum(axis=1, keepdims=True)
    spread[0, 0:ROWS] = jnp.where(lane < 2, 0.0, corner)
    fetches[3].wait()
    columns = []
    for z in range(LAYERS):
        stack = []
        for part in range(2):
            for parity in range(2):
                stack.append(spread[parity, pl.ds(part * LAYERS + z, KEPT // 2, stride=ROWS), :])
        columns.append(jnp.concatenate(stack, 0))
    mixed = dot3((ax[0], ax[1]), split(jnp.concatenate(columns, 1)))
    fields[...] = mixed

    fetches[4].wait()
    fetches[5].wait()
    fetches[6].wait()
    cos_x, sin_x = quarter(lax.broadcasted_iota(jnp.int32, (NG, KEPT), 0))
    cos_y, sin_y = quarter(lax.broadcasted_iota(jnp.int32, (1, NG), 1))
    got_x = jnp.zeros((ROWS, 128), F32)
    got_y = jnp.zeros((ROWS, 128), F32)
    centre = lax.broadcasted_iota(jnp.int32, (1, KEPT), 1) == KEPT // 2
    for z in range(LAYERS):
        re = fields[0:NG, z * KEPT : (z + 1) * KEPT]
        im = fields[NG : 2 * NG, z * KEPT : (z + 1) * KEPT]
        er = jnp.where(centre, edge_x[z : z + 1], 0.0)
        ei = jnp.where(centre, edge_x[LAYERS + z : LAYERS + z + 1], 0.0)
        re = re + (cos_x * er - sin_x * ei)
        im = im + (sin_x * er + cos_x * ei)
        wave = dot3(split(jnp.concatenate([re, im], 1)), (ay[0], ay[1]))
        er = edge_y[z : z + 1]
        ei = edge_y[LAYERS + z : LAYERS + z + 1]
        local = pot[z]
        re = (wave[:, :NG] + (cos_y * er - sin_y * ei)) * local
        im = (wave[:, NG:] + (sin_y * er + cos_y * ei)) * local
        sum_re = re.sum(axis=0, keepdims=True)
        sum_im = im.sum(axis=0, keepdims=True)
        er = (cos_y * sum_re + sin_y * sum_im).sum(axis=1, keepdims=True)
        ei = (cos_y * sum_im - sin_y * sum_re).sum(axis=1, keepdims=True)
        got_y = jnp.where(row_id == z, er, jnp.where(row_id == LAYERS + z, ei, got_y))
        mid = dot3(split(jnp.concatenate([re, im], 1)), (ayt[0], ayt[1]))
        re, im = mid[:, :KEPT], mid[:, KEPT:]
        er = (cos_x * re + sin_x * im).sum(axis=0, keepdims=True)
        ei = (cos_x * im - sin_x * re).sum(axis=0, keepdims=True)
        er = jnp.where(centre, er, 0.0).sum(axis=1, keepdims=True)
        ei = jnp.where(centre, ei, 0.0).sum(axis=1, keepdims=True)
        got_x = jnp.where(row_id == z, er, jnp.where(row_id == LAYERS + z, ei, got_x))
        fields[0:NG, z * KEPT : (z + 1) * KEPT] = re
        fields[NG : 2 * NG, z * KEPT : (z + 1) * KEPT] = im
    fetches[7].wait()
    mixed = dot3((axt[0], axt[1]), split(fields[...]))
    for z in range(LAYERS):
        for part in range(2):
            block = mixed[part * KEPT : (part + 1) * KEPT, z * KEPT : (z + 1) * KEPT]
            for parity in range(2):
                plane[parity, pl.ds(part * LAYERS + z, KEPT // 2, stride=ROWS), :] = block[
                    parity * (KEPT // 2) : (parity + 1) * (KEPT // 2)
                ]
    corner = plane[0, 0:ROWS]
    plane[0, 0:ROWS] = jnp.where(lane == 0, got_x, jnp.where(lane == 1, got_y, corner))
    for parity in range(2):
        high, low = split(plane[parity])
        psi[:, parity * KEPT : (parity + 1) * KEPT] = high
        psi[:, (2 + parity) * KEPT : (3 + parity) * KEPT] = low

    def incoming(ring, spot):
        other = peer(ring, spot, -1)
        return pltpu.make_async_remote_copy(
            src_ref=sback.at[spot_rows(ring * STEP + spot, WIRE)],
            dst_ref=ret.at[spot_rows(me, WIRE)],
            send_sem=rt_send.at[0],
            recv_sem=rt_recv.at[0],
            device_id=(tg, other),
            device_id_type=MESH,
        )

    def pick(turn, carry):
        g = PLANES // STEP - 1 - turn
        tiles = []
        for i in range(0, STEP * 3 // 4, 2):
            right = onehot[g, :, i * 128 : (i + 2) * 128]
            found = dot(psi[...], jnp.concatenate([right, right], 0))
            upper = jnp.concatenate(
                [uppers[g * (STEP * 3 // 4) + i + e] for e in range(2)], 1
            )
            value = jnp.zeros((ROWS, 256), F32)
            for j in range(KEPT // 2):
                value = jnp.where(upper == float(j), found[j * ROWS : (j + 1) * ROWS], value)
            tiles += [value[:, :128], value[:, 128:]]
        for i in range(0, STEP, 4):
            pairs = []
            for a in range(2):
                tile = tiles[i * 3 // 4 + a]
                lower = pltpu.roll(tile, LAYERS, 0)
                pairs.append(jnp.where(half, tile, swap(lower)))
                pairs.append(jnp.where(half, swap(tile), lower))
            tile = tiles[i * 3 // 4 + 2]
            shifts = [tile] + [pltpu.roll(tile, 128 - 32 * d, 1) for d in range(1, 4)]
            for j in range(4):
                turned = by_layer([shifts[(j - b) & 3] for b in range(LAYERS)])
                turned = jnp.where(quad == layer, turned, 0.0)
                re = turned[:LAYERS].sum(axis=0, keepdims=True)
                im = turned[LAYERS:].sum(axis=0, keepdims=True)
                out = jnp.where(sub < LAYERS, pairs[j], jnp.where(sub == LAYERS, re, im))
                sback[spot_rows(g * STEP + i + j, ROWS)] = out
        for i in (4, 5, 6, 7, 2, 3, 1, 0):
            if i > 0:
                incoming(g, i).start()
            else:

                @pl.when(g > 0)
                def _():
                    incoming(g, 0).start()

        return carry

    lax.fori_loop(0, PLANES // STEP, pick, 0)
    ret[spot_rows(me, ROWS)] = sback[0:ROWS]

    height = steps[:DEPTH] + info[2:3]
    height = jnp.where(height >= float(NG), height - float(NG), height)
    height = jnp.where(height >= float(NG // 2), height - float(NG), height)
    kinetic = (0.5 * (32.0 / (NG * NG))) * (info[3:4] + height * height)
    terms[...] = jnp.concatenate([kinetic, kinetic], 0) * masked

    settle(ret.at[pl.ds(0, (PLANES - 1) * WIRE)], rt_recv.at[0])
    fetches[8].wait()
    lead = jnp.concatenate([ret[pl.ds(z, PLANES, stride=ROWS), :] for z in range(LAYERS)], 0)
    lead = lead * phase_a[:NG] + swap(lead) * (phase_a[NG:] * sign)
    rest_re = ret[pl.ds(LAYERS, PLANES, stride=ROWS), :]
    rest_im = ret[pl.ds(LAYERS + 1, PLANES, stride=ROWS), :]
    rest = []
    for value in (
        rest_re * phase_b[0] + rest_im * phase_b[1],
        rest_im * phase_b[0] - rest_re * phase_b[1],
    ):
        rest += [jnp.where(quad1 == b, value, 0.0) for b in range(LAYERS)]
    lead = dot3((lines_t[0, :, :NG], lines_t[1, :, :NG]), split(lead))
    lead = lead[:DEPTH] - swap(lead[DEPTH:]) * sign
    rest = dot3((lines_t[0], lines_t[1]), split(jnp.concatenate(rest, 0)))
    rest = rest + swap(rest)
    rest = rest + pltpu.roll(rest, 32, 1)
    picked = jnp.concatenate(
        [
            jnp.where(half1, lead, rest[:DEPTH]),
            jnp.where(half1, swap(lead), rest[DEPTH:]),
        ],
        0,
    )
    picked = pack(picked, pack_from) + terms[...]
    picked = jnp.where(jnp.concatenate([live, live], 0), picked, 0.0)
    for part in range(2):
        rows = picked[part * DEPTH : (part + 1) * DEPTH].T
        back[part] = rows.reshape(GROUPS, SLOT, DEPTH)

    copies = []
    for step in (2, 1, 3):
        other = (tg + step) & (GROUPS - 1)
        copy = pltpu.make_async_remote_copy(
            src_ref=back.at[:, other],
            dst_ref=result.at[:, tg],
            send_sem=out_send.at[step],
            recv_sem=out_recv.at[step],
            device_id=(other, me),
            device_id_type=MESH,
        )
        copy.start()
        copies.append(copy)
    own = pltpu.make_async_copy(back.at[:, tg], result.at[:, tg], stick_sem.at[0])
    own.start()
    settle(send.at[pl.ds(0, (PLANES - 1) * (WIRE + 1))], pl_send.at[0])
    settle(sback.at[pl.ds(0, (PLANES - 1) * WIRE)], rt_send.at[0])
    own.wait()
    for copy in copies:
        copy.wait()


def local(coeffs, potential, stick_x, stick_y, stick_count, stick_offset):
    consts = [jnp.asarray(t) for t in tables()]
    vmem = lambda *shape, dtype=F32: pltpu.VMEM(shape, dtype)
    dma = pltpu.SemaphoreType.DMA
    args = (coeffs, potential, stick_x, stick_y, stick_count, stick_offset, *consts)
    return pl.pallas_call(
        kernel,
        out_shape=jax.ShapeDtypeStruct((2, GROUPS, SLOT, DEPTH), F32),
        in_specs=[pl.BlockSpec(memory_space=pltpu.HBM)] * len(args),
        out_specs=pl.BlockSpec(memory_space=pltpu.HBM),
        scratch_shapes=[
            vmem(2, GROUPS, SLOT, DEPTH),
            vmem(2, GROUPS, SLOT, DEPTH),
            vmem(4, SLOT, dtype=jnp.int32),
            vmem(8, 128),
            vmem(GROUPS, 8, 128),
            vmem(LAYERS, NG, NG),
        ]
        + [vmem(*t.shape, dtype=BF) for t in consts]
        + [
            vmem(PLANES * ROWS, 128),
            vmem(PLANES * ROWS, 128),
            vmem(2 * NG, 128),
            vmem(2, PLANES, 128),
            vmem(PLANES // STEP, 2 * KEPT, STEP * 96, dtype=BF),
            vmem(2, KEPT // 2 * ROWS, KEPT),
            vmem(2, KEPT // 2 * ROWS, KEPT),
            vmem(KEPT // 2 * ROWS, 4 * KEPT, dtype=BF),
            vmem(2 * NG, LAYERS * KEPT),
            vmem(PLANES * ROWS, 128),
            vmem(PLANES * ROWS, 128),
            vmem(2, GROUPS, SLOT, DEPTH),
            vmem(PLANES * 3 // 4, ROWS, 128),
            vmem(2 * DEPTH, 128),
            dma((4,)),
            dma((10,)),
        ]
        + [dma((GROUPS,))] * 6
        + [dma((1,)), dma((PLANES // STEP,)), dma((1,)), dma((1,))],
        compiler_params=pltpu.CompilerParams(
            collective_id=0, has_side_effects=True, vmem_limit_bytes=62 * 1024 * 1024
        ),
    )(*args)


def solution(mesh):
    in_specs = (
        P(None, None, ("tg", "pl"), None),
        P("pl", None, None),
        P(("tg", "pl")),
        P(("tg", "pl")),
        P(("tg", "pl")),
        P(("tg", "pl")),
    )
    out_specs = P(None, None, ("tg", "pl"), None)
    return jax.shard_map(local, mesh=mesh, in_specs=in_specs, out_specs=out_specs, check_vma=False)
```
